32 devices in a mesh: dp: 2 (over y), pipe: 2 (over x), tensor: 8 (over z, core).
Axes of the slice: x: 2, y: 2, z: 4, core: 2. Of those that a mesh axis runs over, the one named last changes fastest.
Arguments:
- queries: bfloat16 [2, 2, 256, 4096], P('pipe', 'dp', None, 'tensor'), may hold values from -120 to 120
- grad_out: bfloat16 [2, 2, 256, 4096], P('pipe', 'dp', None, 'tensor'), may hold values from -6 to 6
- past_keys: bfloat16 [2, 2, 512, 256], P('pipe', 'dp', 'tensor'), may hold values from -6 to 6
- past_values: bfloat16 [2, 2, 512, 256], P('pipe', 'dp', 'tensor'), may hold values from -6 to 6
- span_keys: bfloat16 [2, 2, 256, 256], P('pipe', 'dp', 'tensor'), may hold values from -6 to 6
- span_values: bfloat16 [2, 2, 256, 256], P('pipe', 'dp', 'tensor'), may hold values from -6 to 6
- normed: bfloat16 [2, 2, 256, 16384], P('pipe', 'dp', None, 'tensor'), may hold values from -6 to 6
- key_weight: bfloat16 [2, 16384, 256], P('pipe', 'tensor'), may hold values from -0.046875 to 0.046875
- value_weight: bfloat16 [2, 16384, 256], P('pipe', 'tensor'), may hold values from -0.046875 to 0.046875
- offsets: int32 [2, 2], P('pipe', 'dp'), may hold values from 256 to 512, as said below
Outputs:
- queries_grad: bfloat16 [2, 2, 256, 4096], P('pipe', 'dp', None, 'tensor')
- past_key_grad: float32 [2, 2, 512, 256], P('pipe', 'dp', 'tensor')
- past_value_grad: float32 [2, 2, 512, 256], P('pipe', 'dp', 'tensor')
- key_weight_grad: float32 [2, 16384, 256], P('pipe', 'tensor', 'dp')
- value_weight_grad: float32 [2, 16384, 256], P('pipe', 'tensor', 'dp')
- section_grad: bfloat16 [2, 2, 256, 16384], P('pipe', 'dp', None, 'tensor')
The draws below stay inside these ranges and needn't reach their ends.
Inputs may be any that keep to these rules, and one draw needn't show every extreme that they name: `offsets`: the number of earlier tokens of that section's sequence that the block's queries see; 256 and 512 are each reached by some section and sequence.
All inputs are finite; a program needn't handle non-finite values.
Results may differ from the reference program's by a relative error of at most 0.014.
The reference program's roundings to bfloat16 on the way count: a program that leaves them out, or rounds other values in their place, can miss the bound.
Values may be sent and summed in bfloat16 or wider, within the bound.
No kernel may reach another device: no remote copies, remote signals or barrier semaphores. Data moves between devices by JAX's collectives and lax.ppermute only.
A program may use at most 64 MiB of HBM per device.

```python
import jax
import jax.numpy as jnp
from jax import lax

D = 16384
HD = 128
GROUP = 16
SPAN = 256
PAST = 512
HEADS = 32
KV_HEADS = 2
SECTIONS = 2
SEQS = 2


def draw_queries(key, part):
    shape = (SECTIONS, SEQS, SPAN, HEADS * HD)
    base_key = jax.random.fold_in(key, 21)
    values = jnp.clip(jax.random.normal(base_key, shape, jnp.float32), -6.0, 6.0)
    return values.astype(jnp.bfloat16)


def draw_grad_out(key, part):
    shape = (SECTIONS, SEQS, SPAN, HEADS * HD)
    base_key = jax.random.fold_in(key, 31)
    values = jnp.clip(jax.random.normal(base_key, shape, jnp.float32), -6.0, 6.0)
    return values.astype(jnp.bfloat16)


def draw_offsets(key, part):
    total_count = SECTIONS * SEQS
    value_key, order_key = jax.random.split(jax.random.fold_in(key, 7))
    flat = jax.random.randint(value_key, (total_count,), PAST // 2, PAST + 1, dtype=jnp.int32)
    order = jax.random.permutation(order_key, total_count)
    flat = flat.at[order[0]].set(PAST).at[order[1]].set(PAST // 2)
    return flat.reshape(SECTIONS, SEQS)


def levels(own_key, shape, shards, low, largest):
    loudness = 1.0
    for axis_at, blocks in shards:
        draws = jax.random.uniform(jax.random.fold_in(jax.random.fold_in(own_key, 6), axis_at), (blocks,), jnp.float32, low / len(shards), largest / len(shards))
        loudness = loudness * jnp.repeat(jnp.exp(draws), shape[axis_at] // blocks).reshape((-1,) + (1,) * (len(shape) - 1 - axis_at))
    return loudness


def noise(stream_key, shape, width, limit, shards=(), kind=jnp.bfloat16):
    values = width * jax.random.normal(stream_key, shape, jnp.float32)
    if shards:
        values = values * levels(stream_key, shape, shards, -0.22, 0.18)
    return jnp.clip(values, -limit, limit).astype(kind)


def setup_inputs(seed: int = 0) -> dict:
    arg_keys = jax.random.split(jax.random.key(seed), 11)
    return {
        "queries": draw_queries(jax.random.fold_in(arg_keys[10], 71), 0),
        "grad_out": draw_grad_out(jax.random.fold_in(arg_keys[10], 71), 0),
        "past_keys": noise(arg_keys[2], (SECTIONS, SEQS, PAST, KV_HEADS * HD), 1.0, 6.0, ((0, 2), (1, 2), (2, 8))),
        "past_values": noise(arg_keys[3], (SECTIONS, SEQS, PAST, KV_HEADS * HD), 1.0, 6.0, ((0, 2), (1, 2), (2, 8))),
        "span_keys": noise(arg_keys[4], (SECTIONS, SEQS, SPAN, KV_HEADS * HD), 1.0, 6.0, ((0, 2), (1, 2), (2, 8))),
        "span_values": noise(arg_keys[5], (SECTIONS, SEQS, SPAN, KV_HEADS * HD), 1.0, 6.0, ((0, 2), (1, 2), (2, 8))),
        "normed": noise(arg_keys[6], (SECTIONS, SEQS, SPAN, D), 1.0, 6.0, ((0, 2), (1, 2), (3, 8))),
        "key_weight": noise(arg_keys[7], (SECTIONS, D, KV_HEADS * HD), D ** -0.5, 0.046875, ((0, 2), (1, 8))),
        "value_weight": noise(arg_keys[8], (SECTIONS, D, KV_HEADS * HD), D ** -0.5, 0.046875, ((0, 2), (1, 8))),
        "offsets": draw_offsets(jax.random.fold_in(arg_keys[10], 71), 0),
    }


rope_base = 500000.0
neg_large = -1e30


def rotary_tables(positions):
    half_dim = HD // 2
    freq_index = jnp.arange(half_dim, dtype=jnp.float32)
    inverse_freq = rope_base ** (-2.0 * freq_index / HD)
    angles = positions.astype(jnp.float32)[:, None] * inverse_freq[None, :]
    return jnp.cos(angles), jnp.sin(angles)


def rotate_rows(values, cosine_table, sine_table):
    half_dim = values.shape[1] // 2
    first_half = values[:, :half_dim]
    second_half = values[:, half_dim:]
    return jnp.concatenate([first_half * cosine_table - second_half * sine_table, second_half * cosine_table + first_half * sine_table], axis=1)


def unrotate_rows(gradient, cosine_table, sine_table):
    half_dim = gradient.shape[1] // 2
    first_grad = gradient[:, :half_dim]
    second_grad = gradient[:, half_dim:]
    return jnp.concatenate([first_grad * cosine_table + second_grad * sine_table, second_grad * cosine_table - first_grad * sine_table], axis=1)


def visible_keys(offset):
    row_index = lax.broadcasted_iota(jnp.int32, (SPAN, PAST + SPAN), 0)
    column_index = lax.broadcasted_iota(jnp.int32, (SPAN, PAST + SPAN), 1)
    return jnp.where(column_index < PAST, column_index < offset, column_index - PAST <= row_index)


def attend_backward(query_rows, grad_rows, key_rows, value_rows, offset):
    positions = jnp.concatenate([jnp.arange(PAST, dtype=jnp.int32), offset + jnp.arange(SPAN, dtype=jnp.int32)])
    cosine_table, sine_table = rotary_tables(positions)
    key_turned = rotate_rows(key_rows.astype(jnp.float32), cosine_table, sine_table).astype(jnp.bfloat16)
    scale_factor = HD ** -0.5
    query_float = query_rows.astype(jnp.float32)
    grad_float = grad_rows.astype(jnp.float32)
    key_float = key_turned.astype(jnp.float32)
    value_float = value_rows.astype(jnp.float32)
    scores = jnp.einsum("thd,kd->htk", query_float, key_float) * scale_factor
    visible = visible_keys(offset)[None]
    masked = jnp.where(visible, scores, neg_large)
    row_max = jnp.max(masked, axis=-1, keepdims=True)
    exponent = jnp.where(visible, jnp.exp(masked - row_max), 0.0)
    attention = exponent / jnp.sum(exponent, axis=-1, keepdims=True)
    attention_bf = attention.astype(jnp.bfloat16)
    attention_back = attention_bf.astype(jnp.float32)
    attended = jnp.einsum("htk,kd->thd", attention_back, value_float)
    row_delta = jnp.sum(grad_float * attended, axis=-1)
    grad_attention = jnp.einsum("thd,kd->htk", grad_float, value_float)
    grad_scores = (attention * (grad_attention - row_delta.T[:, :, None])).astype(jnp.bfloat16)
    score_float = grad_scores.astype(jnp.float32)
    query_grad = (jnp.einsum("htk,kd->thd", score_float, key_float) * scale_factor).astype(jnp.bfloat16)
    key_grad = jnp.einsum("htk,thd->kd", score_float, query_float) * scale_factor
    value_grad = jnp.einsum("htk,thd->kd", attention_back, grad_float)
    key_grad = unrotate_rows(key_grad, cosine_table, sine_table)
    return query_grad, key_grad, value_grad


def reference(queries, grad_out, past_keys, past_values, span_keys, span_values, normed, key_weight, value_weight, offsets):
    query_list, past_key_list, past_value_list, input_list = [], [], [], []
    key_weight_list, value_weight_list = [], []
    for section_index in range(SECTIONS):
        key_total = jnp.zeros((D, KV_HEADS * HD), jnp.float32)
        value_total = jnp.zeros((D, KV_HEADS * HD), jnp.float32)
        section_queries, section_past_keys, section_past_values, section_inputs = [], [], [], []
        for replica in range(SEQS):
            offset = offsets[section_index, replica]
            key_all = jnp.concatenate([past_keys[section_index, replica], span_keys[section_index, replica]], axis=0)
            value_all = jnp.concatenate([past_values[section_index, replica], span_values[section_index, replica]], axis=0)
            query_all = queries[section_index, replica]
            grad_all = grad_out[section_index, replica]

            def per_head(head_index, query_all=query_all, grad_all=grad_all, key_all=key_all, value_all=value_all, offset=offset):
                column_start = head_index * (GROUP * HD)
                query_rows = lax.dynamic_slice_in_dim(query_all, column_start, GROUP * HD, 1).reshape(SPAN, GROUP, HD)
                grad_rows = lax.dynamic_slice_in_dim(grad_all, column_start, GROUP * HD, 1).reshape(SPAN, GROUP, HD)
                key_head = lax.dynamic_slice_in_dim(key_all, head_index * HD, HD, 1)
                value_head = lax.dynamic_slice_in_dim(value_all, head_index * HD, HD, 1)
                return attend_backward(query_rows, grad_rows, key_head, value_head, offset)

            query_grad, key_grad, value_grad = lax.map(per_head, jnp.arange(KV_HEADS, dtype=jnp.int32))
            query_grad = jnp.transpose(query_grad, (1, 0, 2, 3)).reshape(SPAN, HEADS * HD)
            key_flat = jnp.transpose(key_grad, (1, 0, 2)).reshape(PAST + SPAN, KV_HEADS * HD)
            value_flat = jnp.transpose(value_grad, (1, 0, 2)).reshape(PAST + SPAN, KV_HEADS * HD)
            span_key = key_flat[PAST:].astype(jnp.bfloat16)
            span_value = value_flat[PAST:].astype(jnp.bfloat16)
            input_grad = jnp.dot(span_key, key_weight[section_index].T, preferred_element_type=jnp.float32)
            input_grad = input_grad + jnp.dot(span_value, value_weight[section_index].T, preferred_element_type=jnp.float32)
            key_part = jnp.dot(normed[section_index, replica].T, span_key, preferred_element_type=jnp.float32)
            value_part = jnp.dot(normed[section_index, replica].T, span_value, preferred_element_type=jnp.float32)
            key_total = key_total + lax.optimization_barrier(key_part.astype(jnp.bfloat16)).astype(jnp.float32)
            value_total = value_total + lax.optimization_barrier(value_part.astype(jnp.bfloat16)).astype(jnp.float32)
            section_queries.append(query_grad)
            section_past_keys.append(key_flat[:PAST])
            section_past_values.append(value_flat[:PAST])
            section_inputs.append(input_grad.astype(jnp.bfloat16))
        query_list.append(jnp.stack(section_queries))
        past_key_list.append(jnp.stack(section_past_keys))
        past_value_list.append(jnp.stack(section_past_values))
        input_list.append(jnp.stack(section_inputs))
        key_weight_list.append(key_total)
        value_weight_list.append(value_total)
    inputs_all = jnp.stack(input_list)
    section_grad = jnp.concatenate([inputs_all[1:], jnp.zeros_like(inputs_all[:1])], axis=0)
    return (jnp.stack(query_list), jnp.stack(past_key_list), jnp.stack(past_value_list), jnp.stack(key_weight_list), jnp.stack(value_weight_list), section_grad)
```

```python
import functools

import jax
import jax.numpy as jnp
from jax import lax
from jax.experimental import pallas as pl
from jax.experimental.pallas import tpu as pltpu
from jax.sharding import PartitionSpec as P

HD = 128
rope_base = 500000.0
neg_large = -1e30
BF = jnp.bfloat16
F32 = jnp.float32
VMEM = pltpu.VMEM

AHEAD = 8


def call(body, out_shape, args, scratch=(), flops=0, nbytes=0):
    return pl.pallas_call(
        body,
        out_shape=out_shape,
        in_specs=[pl.BlockSpec(memory_space=VMEM)] * len(args),
        out_specs=jax.tree.map(lambda _: pl.BlockSpec(memory_space=VMEM), out_shape),
        scratch_shapes=list(scratch),
        compiler_params=pltpu.CompilerParams(vmem_limit_bytes=40 * 1024 * 1024),
        cost_estimate=pl.CostEstimate(flops=flops, bytes_accessed=nbytes, transcendentals=0),
    )(*args)


def shape(rows, columns, dtype):
    return jax.ShapeDtypeStruct((rows, columns), dtype)


def swap(block, axis, distance):
    size = lax.axis_size(axis)
    return lax.ppermute(block, axis, [(i, i ^ distance) for i in range(size)])


def from_next_section(block):
    size = lax.axis_size("pipe")
    return lax.ppermute(block, "pipe", [(i, i - 1) for i in range(1, size)])


def head_columns(head):
    return pl.ds(pl.multiple_of(head * HD, HD), HD)


def my_place(copies):
    me = lax.axis_index("tensor")
    return me // 2, me % 2, me // copies


def pack_body(heads, copies, pk, pv, sk, sv, *outs):
    z, core, own = my_place(copies)
    rows = pk.shape[0]
    for apart in range(heads):
        columns = head_columns(own ^ apart)
        outs[apart][:rows, :HD] = pk[:, columns]
        outs[apart][:rows, HD:] = pv[:, columns]
        outs[apart][rows:, :HD] = sk[:, columns]
        outs[apart][rows:, HD:] = sv[:, columns]


def attend_body(chips, past_rows, span_rows, q, do, cos, sin, first, *refs):
    pieces = refs[: 2 * chips]
    dq, keep, send, kr, krt, v, at, dst, qs, ds = refs[2 * chips :]
    span = q.shape[0]
    heads = q.shape[1] // HD
    past = 2 * chips * past_rows
    keys = past + 2 * chips * span_rows
    scale = HD**-0.5
    for place in range(2 * chips):
        piece = pieces[place]
        for start, count, lower in (
            (place * past_rows, past_rows, 0),
            (past + place * span_rows, span_rows, past_rows),
        ):
            rows = slice(start, start + count)
            k = piece[lower : lower + count, :HD].astype(F32)
            turned = k * cos[rows, :] + pltpu.roll(k, HD // 2, 1) * sin[rows, :]
            kr[rows, :] = turned.astype(BF)
            v[rows, :] = piece[lower : lower + count, HD:]
    krt[...] = kr[...].T
    for h in range(heads):
        qs[h * span : (h + 1) * span, :] = q[:, h * HD : (h + 1) * HD]
        ds[h * span : (h + 1) * span, :] = do[:, h * HD : (h + 1) * HD]
    row = lax.broadcasted_iota(jnp.int32, (keys, span), 1)
    start_key = jnp.concatenate([first[...]] * (span // HD), axis=1)
    visible = start_key <= row
    contract_last = (((1,), (1,)), ((), ()))
    for h in range(heads):
        columns = slice(h * span, (h + 1) * span)
        s = lax.dot_general(kr[...], qs[columns, :], contract_last, preferred_element_type=F32)
        s = jnp.where(visible, s * scale, neg_large)
        e = jnp.exp(s - jnp.max(s, axis=0, keepdims=True))
        a = e * (1.0 / jnp.sum(e, axis=0, keepdims=True))
        a_bf = a.astype(BF)
        at[:, columns] = a_bf
        dp = lax.dot_general(v[...], ds[columns, :], contract_last, preferred_element_type=F32)
        delta = jnp.sum(a_bf.astype(F32) * dp, axis=0, keepdims=True)
        d = (a * (dp - delta)).astype(BF)
        dst[:, columns] = d
        dqt = jnp.dot(krt[...], d, preferred_element_type=F32) * scale
        dq[:, h * HD : (h + 1) * HD] = dqt.T.astype(BF)
    dk = jnp.dot(dst[...], qs[...], preferred_element_type=F32) * scale
    dk = dk * cos[...] - pltpu.roll(dk, HD // 2, 1) * sin[...]
    dv = jnp.dot(at[...], ds[...], preferred_element_type=F32)
    half = chips * past_rows
    quarter = chips * span_rows
    for columns, grad in ((slice(0, HD), dk), (slice(HD, 2 * HD), dv)):
        keep[:half, columns] = grad[:half]
        keep[half:, columns] = grad[past : past + quarter]
        send[:half, columns] = grad[half:past].astype(BF)
        send[half:, columns] = grad[past + quarter :].astype(BF)


def chip_sum_body(chips, past_rows, keep, received, *outs):
    own, sends = outs[0], outs[1:]
    half = chips * past_rows
    total = keep[...] + received[...].astype(F32)
    own[:past_rows, :] = total[:past_rows]
    own[past_rows:, :] = total[half:]
    span_part = total[half:].astype(BF)
    for j in range(1, chips):
        sends[j - 1][:past_rows, :] = total[j * past_rows : (j + 1) * past_rows].astype(BF)
        sends[j - 1][past_rows:, :] = span_part


def group_sum_body(heads, copies, chips, past_rows, span_rows, peers, *refs):
    own, received = refs[0], refs[1:chips]
    dk_past, dv_past, span_grad = refs[chips : chips + 3]
    sends = refs[chips + 3 : chips + 2 + peers]
    mine, ordered = refs[chips + 2 + peers :]
    z, core, head = my_place(copies)
    replica = lax.axis_index("dp")
    per_head = copies // 2
    width = heads * HD
    share = width // peers
    for apart in range(heads):
        past_total = None
        span_total = [None] * chips
        for j in range(apart * per_head, (apart + 1) * per_head):
            block = own if j == 0 else received[j - 1]
            part = block[:past_rows, :].astype(F32)
            past_total = part if past_total is None else past_total + part
            for i in range(chips):
                lower = past_rows + i * span_rows
                part = block[lower : lower + span_rows, :].astype(F32)
                span_total[i ^ j] = part if span_total[i ^ j] is None else span_total[i ^ j] + part
        columns = head_columns(head ^ apart)
        dk_past[:, columns] = past_total[:, :HD]
        dv_past[:, columns] = past_total[:, HD:]
        value_columns = pl.ds(pl.multiple_of(width + (head ^ apart) * HD, HD), HD)
        for i in range(chips):
            rows = pl.ds(pl.multiple_of((z ^ i) * span_rows, span_rows), span_rows)
            rounded = span_total[i].astype(ordered.dtype)
            ordered[rows, columns] = rounded[:, :HD]
            ordered[rows, value_columns] = rounded[:, HD:]
    span_grad[...] = ordered[...].astype(BF)
    for k in range(peers):
        target = mine if k == 0 else sends[k - 1]
        lower = pl.multiple_of((replica ^ k) * share, HD)
        target[:, :share] = span_grad[:, pl.ds(lower, share)]
        target[:, share:] = span_grad[:, pl.ds(pl.multiple_of(width + lower, HD), share)]


def row_type(span_rows):
    return BF if span_rows % 16 == 0 else F32


def weave(chips, span_rows, target, own, other):
    core = lax.axis_index("tensor") % 2
    for z in range(chips):
        part = slice(z * span_rows, (z + 1) * span_rows)
        lower = pl.multiple_of((2 * z + core) * span_rows, span_rows)
        target[pl.ds(lower, span_rows), :] = own[part, :].astype(target.dtype)
        lower = pl.multiple_of((2 * z + 1 - core) * span_rows, span_rows)
        target[pl.ds(lower, span_rows), :] = other[part, :].astype(target.dtype)


def input_grad_body(chips, span_rows, own, other, kw, vw, out, rows):
    weave(chips, span_rows, rows, own, other)
    width = kw.shape[1]
    contract_last = (((1,), (1,)), ((), ()))
    total = lax.dot_general(rows[:, :width].astype(BF), kw[...], contract_last, preferred_element_type=F32)
    total = total + lax.dot_general(
        rows[:, width:].astype(BF), vw[...], contract_last, preferred_element_type=F32
    )
    out[...] = total.astype(BF)


def weight_grad_body(chips, span_rows, replicas, *refs):
    normed = refs[:replicas]
    own = refs[replicas : 2 * replicas]
    other = refs[2 * replicas : 3 * replicas]
    dkw, dvw, rows = refs[3 * replicas :]
    share = dkw.shape[1]
    contract_first = (((0,), (0,)), ((), ()))
    total = None
    for k in range(replicas):
        weave(chips, span_rows, rows.at[k], own[k], other[k])
        product = lax.dot_general(
            normed[k][...], rows[k].astype(BF), contract_first, preferred_element_type=F32
        )
        product = product.astype(BF).astype(F32)
        total = product if total is None else total + product
    dkw[...] = total[:, :share]
    dvw[...] = total[:, share:]


def key_tables(chips, past_rows, span_rows, offset):
    me = lax.axis_index("tensor")

    def places(rows):
        index = lax.broadcasted_iota(jnp.int32, (2 * chips * rows, HD), 0)
        place = index // rows
        holder = 2 * ((me // 2) ^ (place % chips)) + ((me % 2) ^ (place // chips))
        return holder * rows + index % rows

    past = places(past_rows)
    span = places(span_rows)
    positions = jnp.concatenate([past, offset + span], axis=0)
    first = jnp.concatenate([jnp.where(past < offset, -1, 1 << 30), span], axis=0)
    lane = lax.broadcasted_iota(jnp.int32, positions.shape, 1)
    inverse_freq = rope_base ** (-2.0 * (lane % (HD // 2)).astype(F32) / HD)
    angles = positions.astype(F32) * inverse_freq
    sine = jnp.sin(angles)
    return jnp.cos(angles), jnp.where(lane < HD // 2, -sine, sine), first


def on_device(
    queries,
    grad_out,
    past_keys,
    past_values,
    span_keys,
    span_values,
    normed,
    key_weight,
    value_weight,
    offsets,
):
    devices = lax.axis_size("tensor")
    replicas = lax.axis_size("dp")
    chips = devices // 2
    past_rows = past_keys.shape[2]
    span_rows = span_keys.shape[2]
    span = queries.shape[2]
    width = past_keys.shape[3]
    heads = width // HD
    copies = devices // heads
    features = normed.shape[3]
    share = width // replicas
    keys = devices * (past_rows + span_rows)
    local_heads = queries.shape[3] // HD

    normed_rows = normed[0, 0]
    kw, vw = key_weight[0], value_weight[0]
    ahead = features * AHEAD // 16

    packed = call(
        functools.partial(pack_body, heads, copies),
        [shape(past_rows + span_rows, 2 * HD, BF)] * heads,
        (past_keys[0, 0], past_values[0, 0], span_keys[0, 0], span_values[0, 0]),
        nbytes=2 * (past_rows + span_rows) * 2 * width * 2,
    )
    per_head = copies // 2
    pieces = [packed[0]] + [swap(packed[j // per_head], "tensor", 2 * j) for j in range(1, chips)]
    pieces = pieces + [swap(piece, "tensor", 1) for piece in pieces]

    normed_from = [normed_rows] + [swap(normed_rows, "dp", k) for k in range(1, replicas)]
    kw_ahead = from_next_section(kw[:ahead])
    vw_ahead = from_next_section(vw[:ahead])

    cos, sin, first = key_tables(chips, past_rows, span_rows, offsets[0, 0])
    part_rows = chips * (past_rows + span_rows)
    query_grad, keep, send = call(
        functools.partial(attend_body, chips, past_rows, span_rows),
        [
            shape(span, local_heads * HD, BF),
            shape(part_rows, 2 * HD, F32),
            shape(part_rows, 2 * HD, BF),
        ],
        (queries[0, 0], grad_out[0, 0], cos, sin, first, *pieces),
        scratch=[
            VMEM((keys, HD), BF),
            VMEM((HD, keys), BF),
            VMEM((keys, HD), BF),
            VMEM((keys, local_heads * span), BF),
            VMEM((keys, local_heads * span), BF),
            VMEM((local_heads * span, HD), BF),
            VMEM((local_heads * span, HD), BF),
        ],
        flops=10 * keys * local_heads * span * HD,
        nbytes=4 * span * local_heads * HD * 2,
    )
    own, *sends = call(
        functools.partial(chip_sum_body, chips, past_rows),
        [shape(past_rows + chips * span_rows, 2 * HD, F32)]
        + [shape(past_rows + chips * span_rows, 2 * HD, BF)] * (chips - 1),
        (keep, swap(send, "tensor", 1)),
        nbytes=part_rows * 2 * HD * 8,
    )
    received = [swap(sends[j - 1], "tensor", 2 * j) for j in range(1, chips)]
    dk_past, dv_past, span_grad, *shares = call(
        functools.partial(group_sum_body, heads, copies, chips, past_rows, span_rows, replicas),
        [
            shape(past_rows, width, F32),
            shape(past_rows, width, F32),
            shape(chips * span_rows, 2 * width, BF),
        ]
        + [shape(chips * span_rows, 2 * share, BF)] * replicas,
        (own, *received),
        scratch=[VMEM((chips * span_rows, 2 * width), row_type(span_rows))],
        nbytes=part_rows * 2 * HD * 8,
    )
    next_grad = from_next_section(span_grad)
    share_from = [shares[-1]] + [swap(shares[k - 1], "dp", k) for k in range(1, replicas)]

    late = call(
        functools.partial(input_grad_body, chips, span_rows),
        shape(span, features - ahead, BF),
        (span_grad, swap(span_grad, "tensor", 1), kw[ahead:], vw[ahead:]),
        scratch=[VMEM((span, 2 * width), row_type(span_rows))],
        flops=4 * span * width * (features - ahead),
        nbytes=(features - ahead) * (4 * width + 2 * span),
    )
    late = from_next_section(late)
    early = call(
        functools.partial(input_grad_body, chips, span_rows),
        shape(span, ahead, BF),
        (next_grad, swap(next_grad, "tensor", 1), kw_ahead, vw_ahead),
        scratch=[VMEM((span, 2 * width), row_type(span_rows))],
        flops=4 * span * width * ahead,
        nbytes=ahead * (4 * width + 2 * span),
    )
    dkw, dvw = call(
        functools.partial(weight_grad_body, chips, span_rows, replicas),
        [shape(features, share, F32)] * 2,
        (*normed_from, *share_from, *[swap(part, "tensor", 1) for part in share_from]),
        scratch=[VMEM((replicas, span, 2 * share), row_type(span_rows))],
        flops=4 * span * features * share * replicas,
        nbytes=features * (2 * span * replicas + 8 * share),
    )
    section_grad = jnp.concatenate([early, late], axis=1)
    return (
        query_grad[None, None],
        dk_past[None, None],
        dv_past[None, None],
        dkw[None],
        dvw[None],
        section_grad[None, None],
    )


def solution(mesh):
    return jax.shard_map(
        on_device,
        mesh=mesh,
        in_specs=(
            P("pipe", "dp", None, "tensor"),
            P("pipe", "dp", None, "tensor"),
            P("pipe", "dp", "tensor", None),
            P("pipe", "dp", "tensor", None),
            P("pipe", "dp", "tensor", None),
            P("pipe", "dp", "tensor", None),
            P("pipe", "dp", None, "tensor"),
            P("pipe", "tensor", None),
            P("pipe", "tensor", None),
            P("pipe", "dp"),
        ),
        out_specs=(
            P("pipe", "dp", None, "tensor"),
            P("pipe", "dp", "tensor", None),
            P("pipe", "dp", "tensor", None),
            P("pipe", "tensor", "dp"),
            P("pipe", "tensor", "dp"),
            P("pipe", "dp", None, "tensor"),
        ),
        check_vma=False,
    )
```

```python
import functools

import jax
import jax.numpy as jnp
import numpy as np
from jax import lax
from jax.experimental import pallas as pl
from jax.experimental.pallas import tpu as pltpu
from jax.sharding import PartitionSpec as P

HD = 128
rope_base = 500000.0
neg_large = -1e30
BF = jnp.bfloat16
F32 = jnp.float32
VMEM = pltpu.VMEM

AHEAD = 8


def call(body, out_shape, args, scratch=(), flops=0, nbytes=0, specs=None, limit=40):
    return pl.pallas_call(
        body,
        out_shape=out_shape,
        in_specs=specs or [pl.BlockSpec(memory_space=VMEM)] * len(args),
        out_specs=jax.tree.map(lambda _: pl.BlockSpec(memory_space=VMEM), out_shape),
        scratch_shapes=list(scratch),
        compiler_params=pltpu.CompilerParams(vmem_limit_bytes=limit * 1024 * 1024),
        cost_estimate=pl.CostEstimate(flops=flops, bytes_accessed=nbytes, transcendentals=0),
    )(*args)


def shape(rows, columns, dtype):
    return jax.ShapeDtypeStruct((rows, columns), dtype)


def swap(block, axis, distance):
    size = lax.axis_size(axis)
    return lax.ppermute(block, axis, [(i, i ^ distance) for i in range(size)])


def from_next_section(block):
    size = lax.axis_size("pipe")
    return lax.ppermute(block, "pipe", [(i, (i - 1) % size) for i in range(size)])


def after(block, *events):
    return lax.optimization_barrier((block, *events))[0]


def head_columns(head):
    return pl.ds(pl.multiple_of(head * HD, HD), HD)


def my_place(copies):
    me = lax.axis_index("tensor")
    return me // 2, me % 2, me // copies


def load_all(sources, targets, arrived):
    loads = [
        pltpu.make_async_copy(source, target, arrived.at[i])
        for i, (source, target) in enumerate(zip(sources, targets))
    ]
    for load in loads:
        load.start()
    for load in loads:
        load.wait()


def pack_body(heads, copies, *refs):
    z, core, own = my_place(copies)
    outs, held, arrived = refs[4 : 4 + heads], refs[4 + heads : 8 + heads], refs[-1]
    load_all(refs[:4], held, arrived)
    pk, pv, sk, sv = held
    rows = pk.shape[0]
    for apart in range(heads):
        columns = head_columns(own ^ apart)
        outs[apart][:rows, :HD] = pk[:, columns]
        outs[apart][:rows, HD:] = pv[:, columns]
        outs[apart][rows:, :HD] = sk[:, columns]
        outs[apart][rows:, HD:] = sv[:, columns]


def ahead_body(kw, vw, weights, arrived):
    ahead = weights.shape[0] // 2
    count = arrived.shape[0] // 2
    rows = ahead // count
    sources = [array.at[pl.ds(i * rows, rows)] for array in (kw, vw) for i in range(count)]
    targets = [weights.at[pl.ds(i * rows, rows)] for i in range(2 * count)]
    load_all(sources, targets, arrived)


def table_body(chips, past_rows, span_rows, offset, freq, cos, sin, first):
    me = lax.axis_index("tensor")
    z, core = me // 2, me % 2
    places = 2 * chips
    start = offset[0, 0]
    frequencies = freq[...]
    place = lax.broadcasted_iota(jnp.int32, (places, HD), 0)
    holder = 2 * (z ^ (place % chips)) + (core ^ (place // chips))
    row = lax.broadcasted_iota(jnp.int32, (max(past_rows, span_rows), HD), 0)
    lane = lax.broadcasted_iota(jnp.int32, row.shape, 1)

    def turn(positions):
        angles = positions.astype(F32) * frequencies
        return jnp.cos(angles), jnp.sin(angles)

    row_cos, row_sin = turn(row)
    for low, rows, begin in ((0, past_rows, 0), (places * past_rows, span_rows, start)):
        place_cos, place_sin = turn(begin + rows * holder)
        signs = jnp.where(lane[:rows] < HD // 2, -1.0, 1.0)
        for i in range(places):
            part = slice(low + i * rows, low + (i + 1) * rows)
            c, s = place_cos[i : i + 1], place_sin[i : i + 1]
            cos[part, :] = c * row_cos[:rows] - s * row_sin[:rows]
            sin[part, :] = (s * row_cos[:rows] + c * row_sin[:rows]) * signs
            index = rows * (2 * (z ^ (i % chips)) + (core ^ (i // chips))) + row[:rows]
            first[part, :] = jnp.where(index < start, -1, 1 << 30) if low == 0 else index


def attend_body(chips, past_rows, span_rows, q, do, cos, sin, first, *refs):
    pieces = refs[: 2 * chips]
    dq, keep, send, kr, krt, v, at, dst, qs, ds = refs[2 * chips :]
    span = q.shape[0]
    heads = q.shape[1] // HD
    past = 2 * chips * past_rows
    keys = past + 2 * chips * span_rows
    scale = HD**-0.5
    for place in range(2 * chips):
        piece = pieces[place]
        for start, count, lower in (
            (place * past_rows, past_rows, 0),
            (past + place * span_rows, span_rows, past_rows),
        ):
            rows = slice(start, start + count)
            k = piece[lower : lower + count, :HD].astype(F32)
            turned = k * cos[rows, :] + pltpu.roll(k, HD // 2, 1) * sin[rows, :]
            kr[rows, :] = turned.astype(BF)
            v[rows, :] = piece[lower : lower + count, HD:]
    krt[...] = kr[...].T
    for h in range(heads):
        qs[h * span : (h + 1) * span, :] = q[:, h * HD : (h + 1) * HD]
        ds[h * span : (h + 1) * span, :] = do[:, h * HD : (h + 1) * HD]
    row = lax.broadcasted_iota(jnp.int32, (keys, span), 1)
    start_key = jnp.concatenate([first[...]] * (span // HD), axis=1)
    visible = start_key <= row
    contract_last = (((1,), (1,)), ((), ()))
    for h in range(heads):
        columns = slice(h * span, (h + 1) * span)
        s = lax.dot_general(kr[...], qs[columns, :], contract_last, preferred_element_type=F32)
        s = jnp.where(visible, s * scale, neg_large)
        e = jnp.exp(s - jnp.max(s, axis=0, keepdims=True))
        a = e * (1.0 / jnp.sum(e, axis=0, keepdims=True))
        a_bf = a.astype(BF)
        at[:, columns] = a_bf
        dp = lax.dot_general(v[...], ds[columns, :], contract_last, preferred_element_type=F32)
        delta = jnp.sum(a_bf.astype(F32) * dp, axis=0, keepdims=True)
        d = (a * (dp - delta)).astype(BF)
        dst[:, columns] = d
        dqt = jnp.dot(krt[...], d, preferred_element_type=F32) * scale
        dq[:, h * HD : (h + 1) * HD] = dqt.T.astype(BF)
    dk = jnp.dot(dst[...], qs[...], preferred_element_type=F32) * scale
    dk = dk * cos[...] - pltpu.roll(dk, HD // 2, 1) * sin[...]
    dv = jnp.dot(at[...], ds[...], preferred_element_type=F32)
    half = chips * past_rows
    quarter = chips * span_rows
    for columns, grad in ((slice(0, HD), dk), (slice(HD, 2 * HD), dv)):
        keep[:half, columns] = grad[:half]
        keep[half:, columns] = grad[past : past + quarter]
        send[:half, columns] = grad[half:past].astype(BF)
        send[half:, columns] = grad[past + quarter :].astype(BF)


def chip_sum_body(chips, past_rows, keep, received, span_own, span_send, *past):
    half = chips * past_rows
    total = keep[...] + received[...].astype(F32)
    span_own[...] = total[half:]
    span_send[...] = total[half:].astype(BF)
    for j in range(chips):
        block = total[j * past_rows : (j + 1) * past_rows]
        past[j][...] = block.astype(past[j].dtype)


def sum_span(heads, copies, chips, span_rows, blocks, ordered, span_grad):
    z, core, head = my_place(copies)
    per_head = copies // 2
    width = heads * HD
    for apart in range(heads):
        total = [None] * chips
        for j in range(apart * per_head, (apart + 1) * per_head):
            for i in range(chips):
                part = blocks[j][i * span_rows : (i + 1) * span_rows, :].astype(F32)
                total[i ^ j] = part if total[i ^ j] is None else total[i ^ j] + part
        key_columns = head_columns(head ^ apart)
        value_columns = pl.ds(pl.multiple_of(width + (head ^ apart) * HD, HD), HD)
        for i in range(chips):
            rows = pl.ds(pl.multiple_of((z ^ i) * span_rows, span_rows), span_rows)
            rounded = total[i].astype(ordered.dtype)
            ordered[rows, key_columns] = rounded[:, :HD]
            ordered[rows, value_columns] = rounded[:, HD:]
    span_grad[...] = ordered[...].astype(BF)


def span_sum_body(heads, copies, chips, span_rows, peers, *refs):
    blocks = refs[:chips]
    span_grad = refs[chips]
    sends = refs[chips + 1 : chips + peers]
    mine, ordered = refs[chips + peers :]
    sum_span(heads, copies, chips, span_rows, blocks, ordered, span_grad)
    replica = lax.axis_index("dp")
    width = heads * HD
    share = width // peers
    for k in range(peers):
        target = mine if k == 0 else sends[k - 1]
        lower = pl.multiple_of((replica ^ k) * share, HD)
        target[:, :share] = span_grad[:, pl.ds(lower, share)]
        target[:, share:] = span_grad[:, pl.ds(pl.multiple_of(width + lower, HD), share)]


def past_sum_body(heads, copies, *refs):
    blocks = refs[:-2]
    dk_past, dv_past = refs[-2:]
    z, core, head = my_place(copies)
    per_head = copies // 2
    for apart in range(heads):
        total = blocks[apart * per_head][...].astype(F32)
        for j in range(apart * per_head + 1, (apart + 1) * per_head):
            total = total + blocks[j][...].astype(F32)
        columns = head_columns(head ^ apart)
        dk_past[:, columns] = total[:, :HD]
        dv_past[:, columns] = total[:, HD:]


def row_type(span_rows):
    return BF if span_rows % 16 == 0 else F32


def weave(chips, span_rows, target, own, other):
    core = lax.axis_index("tensor") % 2
    for z in range(chips):
        part = slice(z * span_rows, (z + 1) * span_rows)
        lower = pl.multiple_of((2 * z + core) * span_rows, span_rows)
        target[pl.ds(lower, span_rows), :] = own[part, :].astype(target.dtype)
        lower = pl.multiple_of((2 * z + 1 - core) * span_rows, span_rows)
        target[pl.ds(lower, span_rows), :] = other[part, :].astype(target.dtype)


def late_grad_body(chips, span_rows, own, other, kw, vw, out, rows):
    weave(chips, span_rows, rows, own, other)
    width = kw.shape[1]
    contract_last = (((1,), (1,)), ((), ()))
    total = lax.dot_general(
        rows[:, :width].astype(BF), kw[...], contract_last, preferred_element_type=F32
    )
    total = total + lax.dot_general(
        rows[:, width:].astype(BF), vw[...], contract_last, preferred_element_type=F32
    )
    out[...] = total.astype(BF)


def early_grad_body(chips, span_rows, sections, own, other, weights, late, out, rows):
    weave(chips, span_rows, rows, own, other)
    ahead, width = weights.shape[0] // 2, weights.shape[1]
    contract_last = (((1,), (1,)), ((), ()))
    total = lax.dot_general(
        rows[:, :width].astype(BF), weights[:ahead], contract_last, preferred_element_type=F32
    )
    total = total + lax.dot_general(
        rows[:, width:].astype(BF), weights[ahead:], contract_last, preferred_element_type=F32
    )
    last = lax.axis_index("pipe") == sections - 1

    @pl.when(last)
    def _():
        out[...] = jnp.zeros_like(out)

    @pl.when(jnp.logical_not(last))
    def _():
        out[:, :ahead] = total.astype(BF)
        out[:, ahead:] = late[...]


def weight_grad_body(chips, span_rows, replicas, *refs):
    normed = refs[:replicas]
    own = refs[replicas : 2 * replicas]
    other = refs[2 * replicas : 3 * replicas]
    dkw, dvw, rows = refs[3 * replicas :]
    share = dkw.shape[1]
    contract_first = (((0,), (0,)), ((), ()))
    total = None
    for k in range(replicas):
        weave(chips, span_rows, rows.at[k], own[k], other[k])
        product = lax.dot_general(
            normed[k][...], rows[k].astype(BF), contract_first, preferred_element_type=F32
        )
        product = product.astype(BF).astype(F32)
        total = product if total is None else total + product
    dkw[...] = total[:, :share]
    dvw[...] = total[:, share:]


def on_device(
    queries,
    grad_out,
    past_keys,
    past_values,
    span_keys,
    span_values,
    normed,
    key_weight,
    value_weight,
    offsets,
):
    devices = lax.axis_size("tensor")
    replicas = lax.axis_size("dp")
    chips = devices // 2
    past_rows = past_keys.shape[2]
    span_rows = span_keys.shape[2]
    span = queries.shape[2]
    width = past_keys.shape[3]
    heads = width // HD
    copies = devices // heads
    features = normed.shape[3]
    share = width // replicas
    keys = devices * (past_rows + span_rows)
    local_heads = queries.shape[3] // HD

    normed_rows = normed[0, 0]
    kw, vw = key_weight[0], value_weight[0]
    ahead = features * AHEAD // 16

    packed = call(
        functools.partial(pack_body, heads, copies),
        [shape(past_rows + span_rows, 2 * HD, BF)] * heads,
        (past_keys[0, 0], past_values[0, 0], span_keys[0, 0], span_values[0, 0]),
        nbytes=2 * (past_rows + span_rows) * 2 * width * 2,
        scratch=[VMEM((past_rows, width), BF)] * 2
        + [VMEM((span_rows, width), BF)] * 2
        + [pltpu.SemaphoreType.DMA((4,))],
        specs=[pl.BlockSpec(memory_space=pltpu.HBM)] * 4,
    )
    per_head = copies // 2
    half_dim = HD // 2
    freq = np.tile(rope_base ** (-2.0 * np.arange(half_dim) / HD), 2).astype(np.float32)
    cos, sin, first = call(
        functools.partial(table_body, chips, past_rows, span_rows),
        [shape(keys, HD, F32)] * 2 + [shape(keys, HD, jnp.int32)],
        (offsets, jnp.asarray(freq[None])),
        nbytes=keys * HD * 12,
        specs=[pl.BlockSpec(memory_space=pltpu.SMEM), pl.BlockSpec(memory_space=VMEM)],
    )
    pieces = [swap(packed[j // per_head], "tensor", 2 * j) for j in range(1, chips)]
    late_kw, late_vw, cos, *pieces = lax.optimization_barrier(
        (after(kw, packed[0])[ahead:], after(vw, packed[0])[ahead:], cos, *pieces)
    )
    pieces = [packed[0], *pieces]
    pieces = pieces + [swap(piece, "tensor", 1) for piece in pieces]

    weights = from_next_section(jnp.concatenate([kw[:ahead], vw[:ahead]], axis=0))
    normed_from = [swap(normed_rows, "dp", k) for k in range(1, replicas)]

    part_rows = chips * (past_rows + span_rows)
    query_grad, keep, send = call(
        functools.partial(attend_body, chips, past_rows, span_rows),
        [
            shape(span, local_heads * HD, BF),
            shape(part_rows, 2 * HD, F32),
            shape(part_rows, 2 * HD, BF),
        ],
        (queries[0, 0], grad_out[0, 0], cos, sin, first, *pieces),
        scratch=[
            VMEM((keys, HD), BF),
            VMEM((HD, keys), BF),
            VMEM((keys, HD), BF),
            VMEM((keys, local_heads * span), BF),
            VMEM((keys, local_heads * span), BF),
            VMEM((local_heads * span, HD), BF),
            VMEM((local_heads * span, HD), BF),
        ],
        flops=10 * keys * local_heads * span * HD,
        nbytes=4 * span * local_heads * HD * 2,
    )
    span_own, span_send, *past = call(
        functools.partial(chip_sum_body, chips, past_rows),
        [
            shape(chips * span_rows, 2 * HD, F32),
            shape(chips * span_rows, 2 * HD, BF),
            shape(past_rows, 2 * HD, F32),
        ]
        + [shape(past_rows, 2 * HD, BF)] * (chips - 1),
        (keep, swap(send, "tensor", 1)),
        nbytes=part_rows * 2 * HD * 8,
    )
    received = [swap(span_send, "tensor", 2 * j) for j in range(1, chips)]
    span_grad, *shares = call(
        functools.partial(span_sum_body, heads, copies, chips, span_rows, replicas),
        [shape(chips * span_rows, 2 * width, BF)]
        + [shape(chips * span_rows, 2 * share, BF)] * replicas,
        (after(span_own, weights), *received),
        scratch=[VMEM((chips * span_rows, 2 * width), row_type(span_rows))],
        nbytes=part_rows * 2 * HD * 8,
    )
    share_from = [shares[-1]] + [swap(shares[k - 1], "dp", k) for k in range(1, replicas)]
    next_grad = from_next_section(span_grad)
    past = past[:1] + [swap(after(past[j], next_grad), "tensor", 2 * j) for j in range(1, chips)]
    dkw, dvw = call(
        functools.partial(weight_grad_body, chips, span_rows, replicas),
        [shape(features, share, F32)] * 2,
        (
            normed_rows,
            *normed_from,
            *share_from,
            *[swap(part, "tensor", 1) for part in share_from],
        ),
        scratch=[VMEM((replicas, span, 2 * share), row_type(span_rows))],
        flops=4 * span * features * share * replicas,
        nbytes=features * (2 * span * replicas + 8 * share),
    )
    dk_past, dv_past = call(
        functools.partial(past_sum_body, heads, copies),
        [shape(past_rows, width, F32)] * 2,
        past,
        nbytes=chips * past_rows * 2 * HD * 4,
    )
    late = call(
        functools.partial(late_grad_body, chips, span_rows),
        shape(span, features - ahead, BF),
        (
            span_grad,
            swap(span_grad, "tensor", 1),
            late_kw,
            late_vw,
        ),
        scratch=[VMEM((span, 2 * width), row_type(span_rows))],
        flops=4 * span * width * (features - ahead),
        nbytes=(features - ahead) * (4 * width + 2 * span),
    )
    late = from_next_section(after(late, next_grad, *normed_from))
    section_grad = call(
        functools.partial(early_grad_body, chips, span_rows, lax.axis_size("pipe")),
        shape(span, features, BF),
        (next_grad, swap(next_grad, "tensor", 1), weights, late),
        scratch=[VMEM((span, 2 * width), row_type(span_rows))],
        flops=4 * span * width * ahead,
        nbytes=ahead * (4 * width + 2 * span),
    )
    return (
        query_grad[None, None],
        dk_past[None, None],
        dv_past[None, None],
        dkw[None],
        dvw[None],
        section_grad[None, None],
    )


def solution(mesh):
    return jax.shard_map(
        on_device,
        mesh=mesh,
        in_specs=(
            P("pipe", "dp", None, "tensor"),
            P("pipe", "dp", None, "tensor"),
            P("pipe", "dp", "tensor", None),
            P("pipe", "dp", "tensor", None),
            P("pipe", "dp", "tensor", None),
            P("pipe", "dp", "tensor", None),
            P("pipe", "dp", None, "tensor"),
            P("pipe", "tensor", None),
            P("pipe", "tensor", None),
            P("pipe", "dp"),
        ),
        out_specs=(
            P("pipe", "dp", None, "tensor"),
            P("pipe", "dp", "tensor", None),
            P("pipe", "dp", "tensor", None),
            P("pipe", "tensor", "dp"),
            P("pipe", "tensor", "dp"),
            P("pipe", "dp", None, "tensor"),
        ),
        check_vma=False,
    )
```

```python
import functools

import jax
import jax.numpy as jnp
import numpy as np
from jax import lax
from jax.experimental import pallas as pl
from jax.experimental.pallas import tpu as pltpu
from jax.sharding import PartitionSpec as P

HD = 128
rope_base = 500000.0
neg_large = -1e30
BF = jnp.bfloat16
F32 = jnp.float32
VMEM = pltpu.VMEM

AHEAD, SHARED = 6, 5


def call(body, out_shape, args, scratch=(), flops=0, nbytes=0, specs=None, limit=40):
    return pl.pallas_call(
        body,
        out_shape=out_shape,
        in_specs=specs or [pl.BlockSpec(memory_space=VMEM)] * len(args),
        out_specs=jax.tree.map(lambda _: pl.BlockSpec(memory_space=VMEM), out_shape),
        scratch_shapes=list(scratch),
        compiler_params=pltpu.CompilerParams(vmem_limit_bytes=limit * 1024 * 1024),
        cost_estimate=pl.CostEstimate(flops=flops, bytes_accessed=nbytes, transcendentals=0),
    )(*args)


def shape(rows, columns, dtype):
    return jax.ShapeDtypeStruct((rows, columns), dtype)


def swap(block, axis, distance):
    size = lax.axis_size(axis)
    return lax.ppermute(block, axis, [(i, i ^ distance) for i in range(size)])


def from_next_section(block):
    size = lax.axis_size("pipe")
    return lax.ppermute(block, "pipe", [(i, (i - 1) % size) for i in range(size)])


def after(block, *events):
    return lax.optimization_barrier((block, *events))[0]


def head_columns(head):
    return pl.ds(pl.multiple_of(head * HD, HD), HD)


def my_place(copies):
    me = lax.axis_index("tensor")
    return me // 2, me % 2, me // copies


def load_all(sources, targets, arrived):
    loads = [
        pltpu.make_async_copy(source, target, arrived.at[i])
        for i, (source, target) in enumerate(zip(sources, targets))
    ]
    for load in loads:
        load.start()
    for load in loads:
        load.wait()


def pack_body(heads, copies, *refs):
    z, core, own = my_place(copies)
    outs, held, arrived = refs[4 : 4 + heads], refs[4 + heads : 8 + heads], refs[-1]
    load_all(refs[:4], held, arrived)
    pk, pv, sk, sv = held
    rows = pk.shape[0]
    for apart in range(heads):
        columns = head_columns(own ^ apart)
        outs[apart][:rows, :HD] = pk[:, columns]
        outs[apart][:rows, HD:] = pv[:, columns]
        outs[apart][rows:, :HD] = sk[:, columns]
        outs[apart][rows:, HD:] = sv[:, columns]


def ahead_body(kw, vw, weights, arrived):
    ahead = weights.shape[0] // 2
    count = arrived.shape[0] // 2
    rows = ahead // count
    sources = [array.at[pl.ds(i * rows, rows)] for array in (kw, vw) for i in range(count)]
    targets = [weights.at[pl.ds(i * rows, rows)] for i in range(2 * count)]
    load_all(sources, targets, arrived)


def table_body(chips, past_rows, span_rows, offset, freq, cos, sin, first):
    me = lax.axis_index("tensor")
    z, core = me // 2, me % 2
    places = 2 * chips
    start = offset[0, 0]
    frequencies = freq[...]
    place = lax.broadcasted_iota(jnp.int32, (places, HD), 0)
    holder = 2 * (z ^ (place % chips)) + (core ^ (place // chips))
    row = lax.broadcasted_iota(jnp.int32, (max(past_rows, span_rows), HD), 0)
    lane = lax.broadcasted_iota(jnp.int32, row.shape, 1)

    def turn(positions):
        angles = positions.astype(F32) * frequencies
        return jnp.cos(angles), jnp.sin(angles)

    row_cos, row_sin = turn(row)
    for low, rows, begin in ((0, past_rows, 0), (places * past_rows, span_rows, start)):
        place_cos, place_sin = turn(begin + rows * holder)
        signs = jnp.where(lane[:rows] < HD // 2, -1.0, 1.0)
        for i in range(places):
            part = slice(low + i * rows, low + (i + 1) * rows)
            c, s = place_cos[i : i + 1], place_sin[i : i + 1]
            cos[part, :] = c * row_cos[:rows] - s * row_sin[:rows]
            sin[part, :] = (s * row_cos[:rows] + c * row_sin[:rows]) * signs
            index = rows * (2 * (z ^ (i % chips)) + (core ^ (i // chips))) + row[:rows]
            first[part, :] = jnp.where(index < start, -1, 1 << 30) if low == 0 else index


def attend_body(chips, past_rows, span_rows, q, do, cos, sin, first, *refs):
    pieces = refs[: 2 * chips]
    dq, keep, send, kr, krt, v, at, dst, qs, ds = refs[2 * chips :]
    span = q.shape[0]
    heads = q.shape[1] // HD
    past = 2 * chips * past_rows
    keys = past + 2 * chips * span_rows
    scale = HD**-0.5
    for place in range(2 * chips):
        piece = pieces[place]
        for start, count, lower in (
            (place * past_rows, past_rows, 0),
            (past + place * span_rows, span_rows, past_rows),
        ):
            rows = slice(start, start + count)
            k = piece[lower : lower + count, :HD].astype(F32)
            turned = k * cos[rows, :] + pltpu.roll(k, HD // 2, 1) * sin[rows, :]
            kr[rows, :] = turned.astype(BF)
            v[rows, :] = piece[lower : lower + count, HD:]
    krt[...] = kr[...].T
    for h in range(heads):
        qs[h * span : (h + 1) * span, :] = q[:, h * HD : (h + 1) * HD]
        ds[h * span : (h + 1) * span, :] = do[:, h * HD : (h + 1) * HD]
    row = lax.broadcasted_iota(jnp.int32, (keys, span), 1)
    start_key = jnp.concatenate([first[...]] * (span // HD), axis=1)
    visible = start_key <= row
    contract_last = (((1,), (1,)), ((), ()))

    def products(h):
        columns = slice(h * span, (h + 1) * span)
        s = lax.dot_general(kr[...], qs[columns, :], contract_last, preferred_element_type=F32)
        dp = lax.dot_general(v[...], ds[columns, :], contract_last, preferred_element_type=F32)
        return s, dp

    following = products(0)
    for h in range(heads):
        columns = slice(h * span, (h + 1) * span)
        s, dp = following
        if h + 1 < heads:
            following = products(h + 1)
        s = jnp.where(visible, s * scale, neg_large)
        e = jnp.exp(s - jnp.max(s, axis=0, keepdims=True))
        a = e * (1.0 / jnp.sum(e, axis=0, keepdims=True))
        a_bf = a.astype(BF)
        at[:, columns] = a_bf
        delta = jnp.sum(a_bf.astype(F32) * dp, axis=0, keepdims=True)
        d = (a * (dp - delta)).astype(BF)
        dst[:, columns] = d
        dqt = jnp.dot(krt[...], d, preferred_element_type=F32) * scale
        dq[:, h * HD : (h + 1) * HD] = dqt.T.astype(BF)
    dk = jnp.dot(dst[...], qs[...], preferred_element_type=F32) * scale
    dk = dk * cos[...] - pltpu.roll(dk, HD // 2, 1) * sin[...]
    dv = jnp.dot(at[...], ds[...], preferred_element_type=F32)
    half = chips * past_rows
    quarter = chips * span_rows
    for columns, grad in ((slice(0, HD), dk), (slice(HD, 2 * HD), dv)):
        keep[:half, columns] = grad[:half]
        keep[half:, columns] = grad[past : past + quarter]
        send[:half, columns] = grad[half:past].astype(BF)
        send[half:, columns] = grad[past + quarter :].astype(BF)


def chip_sum_body(chips, past_rows, keep, received, span_own, span_send, *past):
    half = chips * past_rows
    total = keep[...] + received[...].astype(F32)
    span_own[...] = total[half:]
    span_send[...] = total[half:].astype(BF)
    for j in range(chips):
        block = total[j * past_rows : (j + 1) * past_rows]
        past[j][...] = block.astype(past[j].dtype)


def sum_span(heads, copies, chips, span_rows, blocks, ordered, span_grad):
    z, core, head = my_place(copies)
    per_head = copies // 2
    width = heads * HD
    for apart in range(heads):
        total = [None] * chips
        for j in range(apart * per_head, (apart + 1) * per_head):
            for i in range(chips):
                part = blocks[j][i * span_rows : (i + 1) * span_rows, :].astype(F32)
                total[i ^ j] = part if total[i ^ j] is None else total[i ^ j] + part
        key_columns = head_columns(head ^ apart)
        value_columns = pl.ds(pl.multiple_of(width + (head ^ apart) * HD, HD), HD)
        for i in range(chips):
            rows = pl.ds(pl.multiple_of((z ^ i) * span_rows, span_rows), span_rows)
            rounded = total[i].astype(ordered.dtype)
            ordered[rows, key_columns] = rounded[:, :HD]
            ordered[rows, value_columns] = rounded[:, HD:]
    span_grad[...] = ordered[...].astype(BF)


def span_sum_body(heads, copies, chips, span_rows, peers, *refs):
    blocks = refs[:chips]
    span_grad = refs[chips]
    sends, ordered = refs[chips + 1 : -1], refs[-1]
    sum_span(heads, copies, chips, span_rows, blocks, ordered, span_grad)
    replica = lax.axis_index("dp")
    width = heads * HD
    share = width // peers
    for k, target in enumerate(sends, 1):
        lower = pl.multiple_of((replica ^ k) * share, HD)
        target[:, :share] = span_grad[:, pl.ds(lower, share)]
        target[:, share:] = span_grad[:, pl.ds(pl.multiple_of(width + lower, HD), share)]


def past_sum_body(heads, copies, *refs):
    blocks = refs[:-2]
    dk_past, dv_past = refs[-2:]
    z, core, head = my_place(copies)
    per_head = copies // 2
    for apart in range(heads):
        total = blocks[apart * per_head][...].astype(F32)
        for j in range(apart * per_head + 1, (apart + 1) * per_head):
            total = total + blocks[j][...].astype(F32)
        columns = head_columns(head ^ apart)
        dk_past[:, columns] = total[:, :HD]
        dv_past[:, columns] = total[:, HD:]


def row_type(span_rows):
    return BF if span_rows % 16 == 0 else F32


def weave(chips, span_rows, target, own, other):
    core = lax.axis_index("tensor") % 2
    for z in range(chips):
        part = slice(z * span_rows, (z + 1) * span_rows)
        lower = pl.multiple_of((2 * z + core) * span_rows, span_rows)
        target[pl.ds(lower, span_rows), :] = own[part, :].astype(target.dtype)
        lower = pl.multiple_of((2 * z + 1 - core) * span_rows, span_rows)
        target[pl.ds(lower, span_rows), :] = other[part, :].astype(target.dtype)


def late_grad_body(chips, span_rows, own, other, kw, vw, out, rows):
    weave(chips, span_rows, rows, own, other)
    width = kw.shape[1]
    contract_last = (((1,), (1,)), ((), ()))
    total = lax.dot_general(
        rows[:, :width].astype(BF), kw[...], contract_last, preferred_element_type=F32
    )
    total = total + lax.dot_general(
        rows[:, width:].astype(BF), vw[...], contract_last, preferred_element_type=F32
    )
    out[...] = total.astype(BF)


def early_grad_body(chips, span_rows, sections, ahead, own, other, weights, late, *refs):
    more, (out, rows) = refs[:-2], refs[-2:]
    last = lax.axis_index("pipe") == sections - 1
    width = weights.shape[1]
    ready = out.shape[1] - late.shape[1]
    contract_last = (((1,), (1,)), ((), ()))

    @pl.when(last)
    def _():
        out[...] = jnp.zeros_like(out)

    @pl.when(jnp.logical_not(last))
    def _():
        weave(chips, span_rows, rows, own, other)
        kind = lax.axis_index("dp") if more else 0

        def product(which, block):
            columns = pl.ds(pl.multiple_of(which * width, HD), width)
            grad = rows[:, columns].astype(BF)
            return lax.dot_general(grad, block, contract_last, preferred_element_type=F32)

        total = product(kind, weights[:ahead]) + product(1 - kind, weights[ready:])
        out[:, :ahead] = total.astype(BF)
        if more:
            total = product(kind, weights[ahead:ready]) + product(1 - kind, more[0][...])
            out[:, ahead:ready] = total.astype(BF)
        out[:, ready:] = late[...]


def weight_grad_body(chips, span_rows, replicas, *refs):
    count = replicas - 1
    normed = refs[:replicas]
    span_grad, other_grad = refs[replicas : replicas + 2]
    own = refs[replicas + 2 : replicas + 2 + count]
    other = refs[replicas + 2 + count : replicas + 2 + 2 * count]
    dkw, dvw, mine, rows = refs[replicas + 2 + 2 * count :]
    share = dkw.shape[1]
    width = span_grad.shape[1] // 2
    weave(chips, span_rows, mine, span_grad, other_grad)
    lower = pl.multiple_of(lax.axis_index("dp") * share, HD)
    grads = [
        jnp.concatenate(
            [mine[:, pl.ds(half * width + lower, share)].astype(BF) for half in range(2)], axis=1
        )
    ]
    for k in range(count):
        weave(chips, span_rows, rows.at[k], own[k], other[k])
        grads.append(rows[k].astype(BF))
    contract_first = (((0,), (0,)), ((), ()))
    total = None
    for block, grad in zip(normed, grads):
        product = lax.dot_general(block[...], grad, contract_first, preferred_element_type=F32)
        product = product.astype(BF).astype(F32)
        total = product if total is None else total + product
    dkw[...] = total[:, :share]
    dvw[...] = total[:, share:]


def on_device(
    queries,
    grad_out,
    past_keys,
    past_values,
    span_keys,
    span_values,
    normed,
    key_weight,
    value_weight,
    offsets,
):
    devices = lax.axis_size("tensor")
    replicas = lax.axis_size("dp")
    chips = devices // 2
    past_rows = past_keys.shape[2]
    span_rows = span_keys.shape[2]
    span = queries.shape[2]
    width = past_keys.shape[3]
    heads = width // HD
    copies = devices // heads
    features = normed.shape[3]
    share = width // replicas
    keys = devices * (past_rows + span_rows)
    local_heads = queries.shape[3] // HD

    normed_rows = normed[0, 0]
    kw, vw = key_weight[0], value_weight[0]
    ahead, shared = features * AHEAD // 16, features * SHARED // 16
    if replicas != 2:
        ahead, shared = ahead + shared // 2, 0
    late_start = ahead + shared

    packed = call(
        functools.partial(pack_body, heads, copies),
        [shape(past_rows + span_rows, 2 * HD, BF)] * heads,
        (past_keys[0, 0], past_values[0, 0], span_keys[0, 0], span_values[0, 0]),
        nbytes=2 * (past_rows + span_rows) * 2 * width * 2,
        scratch=[VMEM((past_rows, width), BF)] * 2
        + [VMEM((span_rows, width), BF)] * 2
        + [pltpu.SemaphoreType.DMA((4,))],
        specs=[pl.BlockSpec(memory_space=pltpu.HBM)] * 4,
    )
    per_head = copies // 2
    half_dim = HD // 2
    freq = np.tile(rope_base ** (-2.0 * np.arange(half_dim) / HD), 2).astype(np.float32)
    cos, sin, first = call(
        functools.partial(table_body, chips, past_rows, span_rows),
        [shape(keys, HD, F32)] * 2 + [shape(keys, HD, jnp.int32)],
        (offsets, jnp.asarray(freq[None])),
        nbytes=keys * HD * 12,
        specs=[pl.BlockSpec(memory_space=pltpu.SMEM), pl.BlockSpec(memory_space=VMEM)],
    )
    pieces = [swap(packed[j // per_head], "tensor", 2 * j) for j in range(1, chips)]
    late_kw, late_vw, cos, *pieces = lax.optimization_barrier(
        (after(kw, packed[0])[late_start:], after(vw, packed[0])[late_start:], cos, *pieces)
    )
    pieces = [packed[0], *pieces]
    pieces = pieces + [swap(piece, "tensor", 1) for piece in pieces]

    ready = [kw[:late_start], vw[:ahead]]
    if shared:
        first_half = lax.axis_index("dp") == 0
        ready = [
            jnp.where(first_half, kw[:late_start], vw[:late_start]),
            jnp.where(first_half, vw[:ahead], kw[:ahead]),
        ]
    weights = from_next_section(jnp.concatenate(ready, axis=0))
    normed_from = [swap(normed_rows, "dp", k) for k in range(1, replicas)]

    part_rows = chips * (past_rows + span_rows)
    query_grad, keep, send = call(
        functools.partial(attend_body, chips, past_rows, span_rows),
        [
            shape(span, local_heads * HD, BF),
            shape(part_rows, 2 * HD, F32),
            shape(part_rows, 2 * HD, BF),
        ],
        (queries[0, 0], grad_out[0, 0], cos, sin, first, *pieces),
        scratch=[
            VMEM((keys, HD), BF),
            VMEM((HD, keys), BF),
            VMEM((keys, HD), BF),
            VMEM((keys, local_heads * span), BF),
            VMEM((keys, local_heads * span), BF),
            VMEM((local_heads * span, HD), BF),
            VMEM((local_heads * span, HD), BF),
        ],
        flops=10 * keys * local_heads * span * HD,
        nbytes=4 * span * local_heads * HD * 2,
    )
    span_own, span_send, *past = call(
        functools.partial(chip_sum_body, chips, past_rows),
        [
            shape(chips * span_rows, 2 * HD, F32),
            shape(chips * span_rows, 2 * HD, BF),
            shape(past_rows, 2 * HD, F32),
        ]
        + [shape(past_rows, 2 * HD, BF)] * (chips - 1),
        (keep, swap(send, "tensor", 1)),
        nbytes=part_rows * 2 * HD * 8,
    )
    received = [swap(span_send, "tensor", 2 * j) for j in range(1, chips)]
    span_grad, *shares = call(
        functools.partial(span_sum_body, heads, copies, chips, span_rows, replicas),
        [shape(chips * span_rows, 2 * width, BF)]
        + [shape(chips * span_rows, 2 * share, BF)] * (replicas - 1),
        (after(span_own, weights, *normed_from), *received),
        scratch=[VMEM((chips * span_rows, 2 * width), row_type(span_rows))],
        nbytes=part_rows * 2 * HD * 8,
    )
    share_from = [swap(block, "dp", k + 1) for k, block in enumerate(shares)]
    next_grad = from_next_section(span_grad)
    past = past[:1] + [swap(after(past[j], span_grad if j <= 2 else next_grad), "tensor", 2 * j) for j in range(1, chips)]
    other_grad = swap(span_grad, "tensor", 1)
    dkw, dvw = call(
        functools.partial(weight_grad_body, chips, span_rows, replicas),
        [shape(features, share, F32)] * 2,
        (
            normed_rows,
            *normed_from,
            span_grad,
            other_grad,
            *share_from,
            *[swap(after(part, *normed_from), "tensor", 1) for part in share_from],
        ),
        scratch=[
            VMEM((span, 2 * width), row_type(span_rows)),
            VMEM((replicas - 1, span, 2 * share), row_type(span_rows)),
        ],
        flops=4 * span * features * share * replicas,
        nbytes=features * (2 * span * replicas + 8 * share),
    )
    dk_past, dv_past = call(
        functools.partial(past_sum_body, heads, copies),
        [shape(past_rows, width, F32)] * 2,
        past,
        nbytes=chips * past_rows * 2 * HD * 4,
    )
    late = call(
        functools.partial(late_grad_body, chips, span_rows),
        shape(span, features - late_start, BF),
        (
            span_grad,
            other_grad,
            late_kw,
            late_vw,
        ),
        scratch=[VMEM((span, 2 * width), row_type(span_rows))],
        flops=4 * span * width * (features - late_start),
        nbytes=(features - late_start) * (4 * width + 2 * span),
    )
    more = [swap(after(weights, *share_from)[ahead:late_start], "dp", 1)] if shared else []
    late = from_next_section(after(late, next_grad, past[1], past[2], *share_from))
    section_grad = call(
        functools.partial(early_grad_body, chips, span_rows, lax.axis_size("pipe"), ahead),
        shape(span, features, BF),
        (next_grad, swap(next_grad, "tensor", 1), weights, late, *more),
        scratch=[VMEM((span, 2 * width), row_type(span_rows))],
        flops=4 * span * width * late_start,
        nbytes=late_start * (4 * width + 2 * span),
    )
    return (
        query_grad[None, None],
        dk_past[None, None],
        dv_past[None, None],
        dkw[None],
        dvw[None],
        section_grad[None, None],
    )


def solution(mesh):
    return jax.shard_map(
        on_device,
        mesh=mesh,
        in_specs=(
            P("pipe", "dp", None, "tensor"),
            P("pipe", "dp", None, "tensor"),
            P("pipe", "dp", "tensor", None),
            P("pipe", "dp", "tensor", None),
            P("pipe", "dp", "tensor", None),
            P("pipe", "dp", "tensor", None),
            P("pipe", "dp", None, "tensor"),
            P("pipe", "tensor", None),
            P("pipe", "tensor", None),
            P("pipe", "dp"),
        ),
        out_specs=(
            P("pipe", "dp", None, "tensor"),
            P("pipe", "dp", "tensor", None),
            P("pipe", "dp", "tensor", None),
            P("pipe", "tensor", "dp"),
            P("pipe", "tensor", "dp"),
            P("pipe", "dp", None, "tensor"),
        ),
        check_vma=False,
    )
```

```python
import functools

import jax
import jax.numpy as jnp
import numpy as np
from jax import lax
from jax.experimental import pallas as pl
from jax.experimental.pallas import tpu as pltpu
from jax.sharding import PartitionSpec as P

HD = 128
rope_base = 500000.0
neg_large = -1e30
BF = jnp.bfloat16
F32 = jnp.float32
VMEM = pltpu.VMEM

AHEAD, SHARED = 6, 5


def call(body, out_shape, args, scratch=(), flops=0, nbytes=0, specs=None, limit=40, out_space=VMEM):
    return pl.pallas_call(
        body,
        out_shape=out_shape,
        in_specs=specs or [pl.BlockSpec(memory_space=VMEM)] * len(args),
        out_specs=jax.tree.map(lambda _: pl.BlockSpec(memory_space=out_space), out_shape),
        scratch_shapes=list(scratch),
        compiler_params=pltpu.CompilerParams(vmem_limit_bytes=limit * 1024 * 1024),
        cost_estimate=pl.CostEstimate(flops=flops, bytes_accessed=nbytes, transcendentals=0),
    )(*args)


def shape(rows, columns, dtype):
    return jax.ShapeDtypeStruct((rows, columns), dtype)


def swap(block, axis, distance):
    size = lax.axis_size(axis)
    return lax.ppermute(block, axis, [(i, i ^ distance) for i in range(size)])


def from_next_section(block):
    size = lax.axis_size("pipe")
    return lax.ppermute(block, "pipe", [(i, (i - 1) % size) for i in range(size)])


def after(block, *events):
    return lax.optimization_barrier((block, *events))[0]


def head_columns(head):
    return pl.ds(pl.multiple_of(head * HD, HD), HD)


def my_place(copies):
    me = lax.axis_index("tensor")
    return me // 2, me % 2, me // copies


def load_all(sources, targets, arrived):
    loads = [
        pltpu.make_async_copy(source, target, arrived.at[i])
        for i, (source, target) in enumerate(zip(sources, targets))
    ]
    for load in loads:
        load.start()
    for load in loads:
        load.wait()


def pack_body(heads, copies, *refs):
    z, core, own = my_place(copies)
    outs, held, arrived = refs[4 : 4 + heads], refs[4 + heads : 8 + heads], refs[-1]
    load_all(refs[:4], held, arrived)
    pk, pv, sk, sv = held
    rows = pk.shape[0]
    for apart in range(heads):
        columns = head_columns(own ^ apart)
        outs[apart][:rows, :HD] = pk[:, columns]
        outs[apart][:rows, HD:] = pv[:, columns]
        outs[apart][rows:, :HD] = sk[:, columns]
        outs[apart][rows:, HD:] = sv[:, columns]


def ahead_body(kw, vw, weights, arrived):
    ahead = weights.shape[0] // 2
    count = arrived.shape[0] // 2
    rows = ahead // count
    sources = [array.at[pl.ds(i * rows, rows)] for array in (kw, vw) for i in range(count)]
    targets = [weights.at[pl.ds(i * rows, rows)] for i in range(2 * count)]
    load_all(sources, targets, arrived)


def table_body(chips, past_rows, span_rows, offset, freq, cos, sin, first):
    me = lax.axis_index("tensor")
    z, core = me // 2, me % 2
    places = 2 * chips
    start = offset[0, 0]
    frequencies = freq[...]
    place = lax.broadcasted_iota(jnp.int32, (places, HD), 0)
    holder = 2 * (z ^ (place % chips)) + (core ^ (place // chips))
    row = lax.broadcasted_iota(jnp.int32, (max(past_rows, span_rows), HD), 0)
    lane = lax.broadcasted_iota(jnp.int32, row.shape, 1)

    def turn(positions):
        angles = positions.astype(F32) * frequencies
        return jnp.cos(angles), jnp.sin(angles)

    row_cos, row_sin = turn(row)
    for low, rows, begin in ((0, past_rows, 0), (places * past_rows, span_rows, start)):
        place_cos, place_sin = turn(begin + rows * holder)
        signs = jnp.where(lane[:rows] < HD // 2, -1.0, 1.0)
        for i in range(places):
            part = slice(low + i * rows, low + (i + 1) * rows)
            c, s = place_cos[i : i + 1], place_sin[i : i + 1]
            cos[part, :] = c * row_cos[:rows] - s * row_sin[:rows]
            sin[part, :] = (s * row_cos[:rows] + c * row_sin[:rows]) * signs
            index = rows * (2 * (z ^ (i % chips)) + (core ^ (i // chips))) + row[:rows]
            first[part, :] = jnp.where(index < start, -1, 1 << 30) if low == 0 else index


def attend_body(chips, past_rows, span_rows, q, do, cos, sin, first, *refs):
    pieces = refs[: 2 * chips]
    dq, keep, send, kr, krt, v, at, dst, qs, ds = refs[2 * chips :]
    span = q.shape[0]
    heads = q.shape[1] // HD
    past = 2 * chips * past_rows
    keys = past + 2 * chips * span_rows
    scale = HD**-0.5
    for place in range(2 * chips):
        piece = pieces[place]
        for start, count, lower in (
            (place * past_rows, past_rows, 0),
            (past + place * span_rows, span_rows, past_rows),
        ):
            rows = slice(start, start + count)
            k = piece[lower : lower + count, :HD].astype(F32)
            turned = k * cos[rows, :] + pltpu.roll(k, HD // 2, 1) * sin[rows, :]
            kr[rows, :] = turned.astype(BF)
            v[rows, :] = piece[lower : lower + count, HD:]
    krt[...] = kr[...].T
    for h in range(heads):
        qs[h * span : (h + 1) * span, :] = q[:, h * HD : (h + 1) * HD]
        ds[h * span : (h + 1) * span, :] = do[:, h * HD : (h + 1) * HD]
    row = lax.broadcasted_iota(jnp.int32, (keys, span), 1)
    start_key = jnp.concatenate([first[...]] * (span // HD), axis=1)
    bias = jnp.where(start_key <= row, 0.0, neg_large)
    contract_last = (((1,), (1,)), ((), ()))

    def products(h):
        columns = slice(h * span, (h + 1) * span)
        s = lax.dot_general(kr[...], qs[columns, :], contract_last, preferred_element_type=F32)
        dp = lax.dot_general(v[...], ds[columns, :], contract_last, preferred_element_type=F32)
        return s, dp

    following = products(0)
    for h in range(heads):
        columns = slice(h * span, (h + 1) * span)
        s, dp = following
        if h + 1 < heads:
            following = products(h + 1)
        s = s * scale + bias
        e = jnp.exp(s - jnp.max(s, axis=0, keepdims=True))
        a = e * (1.0 / jnp.sum(e, axis=0, keepdims=True))
        a_bf = a.astype(BF)
        at[:, columns] = a_bf
        delta = jnp.sum(a_bf.astype(F32) * dp, axis=0, keepdims=True)
        d = (a * (dp - delta)).astype(BF)
        dst[:, columns] = d
        dqt = jnp.dot(krt[...], d, preferred_element_type=F32) * scale
        dq[:, h * HD : (h + 1) * HD] = dqt.T.astype(BF)
    dk = jnp.dot(dst[...], qs[...], preferred_element_type=F32) * scale
    dk = dk * cos[...] - pltpu.roll(dk, HD // 2, 1) * sin[...]
    dv = jnp.dot(at[...], ds[...], preferred_element_type=F32)
    half = chips * past_rows
    quarter = chips * span_rows
    for columns, grad in ((slice(0, HD), dk), (slice(HD, 2 * HD), dv)):
        keep[:half, columns] = grad[:half]
        keep[half:, columns] = grad[past : past + quarter]
        send[:half, columns] = grad[half:past].astype(BF)
        send[half:, columns] = grad[past + quarter :].astype(BF)


def chip_sum_body(chips, past_rows, keep, received, span_own, span_send, *past):
    half = chips * past_rows
    total = keep[...] + received[...].astype(F32)
    span_own[...] = total[half:]
    span_send[...] = total[half:].astype(BF)
    for j in range(chips):
        block = total[j * past_rows : (j + 1) * past_rows]
        past[j][...] = block.astype(past[j].dtype)


def sum_span(heads, copies, chips, span_rows, blocks, ordered, span_grad):
    z, core, head = my_place(copies)
    per_head = copies // 2
    width = heads * HD
    for apart in range(heads):
        total = [None] * chips
        for j in range(apart * per_head, (apart + 1) * per_head):
            for i in range(chips):
                part = blocks[j][i * span_rows : (i + 1) * span_rows, :].astype(F32)
                total[i ^ j] = part if total[i ^ j] is None else total[i ^ j] + part
        key_columns = head_columns(head ^ apart)
        value_columns = pl.ds(pl.multiple_of(width + (head ^ apart) * HD, HD), HD)
        for i in range(chips):
            rows = pl.ds(pl.multiple_of((z ^ i) * span_rows, span_rows), span_rows)
            rounded = total[i].astype(ordered.dtype)
            ordered[rows, key_columns] = rounded[:, :HD]
            ordered[rows, value_columns] = rounded[:, HD:]
    span_grad[...] = ordered[...].astype(BF)


def span_sum_body(heads, copies, chips, span_rows, peers, *refs):
    blocks = refs[:chips]
    span_grad = refs[chips]
    sends, ordered = refs[chips + 1 : -1], refs[-1]
    sum_span(heads, copies, chips, span_rows, blocks, ordered, span_grad)
    replica = lax.axis_index("dp")
    width = heads * HD
    share = width // peers
    for k, target in enumerate(sends, 1):
        lower = pl.multiple_of((replica ^ k) * share, HD)
        target[:, :share] = span_grad[:, pl.ds(lower, share)]
        target[:, share:] = span_grad[:, pl.ds(pl.multiple_of(width + lower, HD), share)]


def past_sum_body(heads, copies, *refs):
    blocks = refs[:-2]
    dk_past, dv_past = refs[-2:]
    z, core, head = my_place(copies)
    per_head = copies // 2
    for apart in range(heads):
        total = blocks[apart * per_head][...].astype(F32)
        for j in range(apart * per_head + 1, (apart + 1) * per_head):
            total = total + blocks[j][...].astype(F32)
        columns = head_columns(head ^ apart)
        dk_past[:, columns] = total[:, :HD]
        dv_past[:, columns] = total[:, HD:]


def row_type(span_rows):
    return BF if span_rows % 16 == 0 else F32


def weave(chips, span_rows, target, own, other):
    core = lax.axis_index("tensor") % 2
    for z in range(chips):
        part = slice(z * span_rows, (z + 1) * span_rows)
        lower = pl.multiple_of((2 * z + core) * span_rows, span_rows)
        target[pl.ds(lower, span_rows), :] = own[part, :].astype(target.dtype)
        lower = pl.multiple_of((2 * z + 1 - core) * span_rows, span_rows)
        target[pl.ds(lower, span_rows), :] = other[part, :].astype(target.dtype)


def late_grad_body(chips, span_rows, own, other, kw, vw, out, rows):
    weave(chips, span_rows, rows, own, other)
    width = kw.shape[1]
    contract_last = (((1,), (1,)), ((), ()))
    total = lax.dot_general(
        rows[:, :width].astype(BF), kw[...], contract_last, preferred_element_type=F32
    )
    total = total + lax.dot_general(
        rows[:, width:].astype(BF), vw[...], contract_last, preferred_element_type=F32
    )
    out[...] = total.astype(BF)


def early_grad_body(chips, span_rows, sections, ahead, own, other, weights, late, *refs):
    more, (out, rows, held, held_more, moved) = refs[:-5], refs[-5:]
    last = lax.axis_index("pipe") == sections - 1
    width = weights.shape[1]
    features = held.shape[1]
    ready = features - late.shape[1]
    contract_last = (((1,), (1,)), ((), ()))

    def move(source, low, high, which):
        columns = pl.ds(low, high - low)
        return pltpu.make_async_copy(source, out.at[:, columns], moved.at[which])

    @pl.when(last)
    def _():
        held[...] = jnp.zeros_like(held)
        whole = move(held, 0, features, 0)
        whole.start()
        whole.wait()

    @pl.when(jnp.logical_not(last))
    def _():
        moves = [move(late, ready, features, 0)]
        moves[0].start()
        weave(chips, span_rows, rows, own, other)
        kind = lax.axis_index("dp") if more else 0

        def product(which, block):
            columns = pl.ds(pl.multiple_of(which * width, HD), width)
            grad = rows[:, columns].astype(BF)
            return lax.dot_general(grad, block, contract_last, preferred_element_type=F32)

        total = product(kind, weights[:ahead]) + product(1 - kind, weights[ready:])
        held[:, :ahead] = total.astype(BF)
        moves.append(move(held.at[:, pl.ds(0, ahead)], 0, ahead, 1))
        moves[1].start()
        if more:
            total = product(kind, weights[ahead:ready]) + product(1 - kind, more[0][...])
            held_more[...] = total.astype(BF)
            moves.append(move(held_more, ahead, ready, 2))
            moves[2].start()
        for each in moves:
            each.wait()


def weight_grad_body(chips, span_rows, replicas, *refs):
    count = replicas - 1
    normed = refs[:replicas]
    span_grad, other_grad = refs[replicas : replicas + 2]
    own = refs[replicas + 2 : replicas + 2 + count]
    other = refs[replicas + 2 + count : replicas + 2 + 2 * count]
    dkw, dvw, mine, rows = refs[replicas + 2 + 2 * count :]
    share = dkw.shape[1]
    width = span_grad.shape[1] // 2
    weave(chips, span_rows, mine, span_grad, other_grad)
    lower = pl.multiple_of(lax.axis_index("dp") * share, HD)
    grads = [
        jnp.concatenate(
            [mine[:, pl.ds(half * width + lower, share)].astype(BF) for half in range(2)], axis=1
        )
    ]
    for k in range(count):
        weave(chips, span_rows, rows.at[k], own[k], other[k])
        grads.append(rows[k].astype(BF))
    contract_first = (((0,), (0,)), ((), ()))
    total = None
    for block, grad in zip(normed, grads):
        product = lax.dot_general(block[...], grad, contract_first, preferred_element_type=F32)
        product = product.astype(BF).astype(F32)
        total = product if total is None else total + product
    dkw[...] = total[:, :share]
    dvw[...] = total[:, share:]


def on_device(
    queries,
    grad_out,
    past_keys,
    past_values,
    span_keys,
    span_values,
    normed,
    key_weight,
    value_weight,
    offsets,
):
    devices = lax.axis_size("tensor")
    replicas = lax.axis_size("dp")
    chips = devices // 2
    past_rows = past_keys.shape[2]
    span_rows = span_keys.shape[2]
    span = queries.shape[2]
    width = past_keys.shape[3]
    heads = width // HD
    copies = devices // heads
    features = normed.shape[3]
    share = width // replicas
    keys = devices * (past_rows + span_rows)
    local_heads = queries.shape[3] // HD

    normed_rows = normed[0, 0]
    kw, vw = key_weight[0], value_weight[0]
    ahead, shared = features * AHEAD // 16, features * SHARED // 16
    if replicas != 2:
        ahead, shared = (ahead + shared // 2) // HD * HD, 0
    late_start = ahead + shared

    packed = call(
        functools.partial(pack_body, heads, copies),
        [shape(past_rows + span_rows, 2 * HD, BF)] * heads,
        (past_keys[0, 0], past_values[0, 0], span_keys[0, 0], span_values[0, 0]),
        nbytes=2 * (past_rows + span_rows) * 2 * width * 2,
        scratch=[VMEM((past_rows, width), BF)] * 2
        + [VMEM((span_rows, width), BF)] * 2
        + [pltpu.SemaphoreType.DMA((4,))],
        specs=[pl.BlockSpec(memory_space=pltpu.HBM)] * 4,
    )
    per_head = copies // 2
    half_dim = HD // 2
    freq = np.tile(rope_base ** (-2.0 * np.arange(half_dim) / HD), 2).astype(np.float32)
    cos, sin, first = call(
        functools.partial(table_body, chips, past_rows, span_rows),
        [shape(keys, HD, F32)] * 2 + [shape(keys, HD, jnp.int32)],
        (offsets, jnp.asarray(freq[None])),
        nbytes=keys * HD * 12,
        specs=[pl.BlockSpec(memory_space=pltpu.SMEM), pl.BlockSpec(memory_space=VMEM)],
    )
    pieces = [swap(packed[j // per_head], "tensor", 2 * j) for j in range(1, chips)]
    late_kw, late_vw, cos, *near = lax.optimization_barrier(
        (
            after(kw, packed[0])[late_start:],
            after(vw, packed[0])[late_start:],
            cos,
            packed[0],
            *pieces[:-1],
        )
    )
    pieces = [*near, pieces[-1]]
    pieces = pieces + [swap(piece, "tensor", 1) for piece in pieces]

    ready = [kw[:late_start], vw[:ahead]]
    if shared:
        first_half = lax.axis_index("dp") == 0
        ready = [
            jnp.where(first_half, kw[:late_start], vw[:late_start]),
            jnp.where(first_half, vw[:ahead], kw[:ahead]),
        ]
    weights = from_next_section(jnp.concatenate(ready, axis=0))
    normed_from = [swap(normed_rows, "dp", k) for k in range(1, replicas)]

    part_rows = chips * (past_rows + span_rows)
    query_grad, keep, send = call(
        functools.partial(attend_body, chips, past_rows, span_rows),
        [
            shape(span, local_heads * HD, BF),
            shape(part_rows, 2 * HD, F32),
            shape(part_rows, 2 * HD, BF),
        ],
        (queries[0, 0], grad_out[0, 0], cos, sin, first, *pieces),
        scratch=[
            VMEM((keys, HD), BF),
            VMEM((HD, keys), BF),
            VMEM((keys, HD), BF),
            VMEM((keys, local_heads * span), BF),
            VMEM((keys, local_heads * span), BF),
            VMEM((local_heads * span, HD), BF),
            VMEM((local_heads * span, HD), BF),
        ],
        flops=10 * keys * local_heads * span * HD,
        nbytes=4 * span * local_heads * HD * 2,
    )
    span_own, span_send, *past = call(
        functools.partial(chip_sum_body, chips, past_rows),
        [
            shape(chips * span_rows, 2 * HD, F32),
            shape(chips * span_rows, 2 * HD, BF),
            shape(past_rows, 2 * HD, F32),
        ]
        + [shape(past_rows, 2 * HD, BF)] * (chips - 1),
        (keep, swap(send, "tensor", 1)),
        nbytes=part_rows * 2 * HD * 8,
    )
    received = [swap(span_send, "tensor", 2 * j) for j in range(1, chips)]
    span_grad, *shares = call(
        functools.partial(span_sum_body, heads, copies, chips, span_rows, replicas),
        [shape(chips * span_rows, 2 * width, BF)]
        + [shape(chips * span_rows, 2 * share, BF)] * (replicas - 1),
        (after(span_own, weights, *normed_from), *received),
        scratch=[VMEM((chips * span_rows, 2 * width), row_type(span_rows))],
        nbytes=part_rows * 2 * HD * 8,
    )
    share_from = [swap(block, "dp", k + 1) for k, block in enumerate(shares)]
    next_grad = from_next_section(span_grad)
    past = past[:1] + [swap(after(past[j], span_grad if j <= 2 else next_grad), "tensor", 2 * j) for j in range(1, chips)]
    other_grad = swap(span_grad, "tensor", 1)
    dkw, dvw = call(
        functools.partial(weight_grad_body, chips, span_rows, replicas),
        [shape(features, share, F32)] * 2,
        (
            normed_rows,
            *normed_from,
            span_grad,
            other_grad,
            *share_from,
            *[swap(after(part, *normed_from), "tensor", 1) for part in share_from],
        ),
        scratch=[
            VMEM((span, 2 * width), row_type(span_rows)),
            VMEM((replicas - 1, span, 2 * share), row_type(span_rows)),
        ],
        flops=4 * span * features * share * replicas,
        nbytes=features * (2 * span * replicas + 8 * share),
    )
    dk_past, dv_past = call(
        functools.partial(past_sum_body, heads, copies),
        [shape(past_rows, width, F32)] * 2,
        past,
        nbytes=chips * past_rows * 2 * HD * 4,
    )
    late = call(
        functools.partial(late_grad_body, chips, span_rows),
        shape(span, features - late_start, BF),
        (
            span_grad,
            other_grad,
            late_kw,
            late_vw,
        ),
        scratch=[VMEM((span, 2 * width), row_type(span_rows))],
        flops=4 * span * width * (features - late_start),
        nbytes=(features - late_start) * (4 * width + 2 * span),
    )
    more = [swap(after(weights, *share_from)[ahead:late_start], "dp", 1)] if shared else []
    late = from_next_section(after(late, next_grad, past[1], past[2], *share_from))
    section_grad = call(
        functools.partial(early_grad_body, chips, span_rows, lax.axis_size("pipe"), ahead),
        shape(span, features, BF),
        (next_grad, swap(next_grad, "tensor", 1), weights, late, *more),
        scratch=[
            VMEM((span, 2 * width), row_type(span_rows)),
            VMEM((span, features), BF),
            VMEM((span, shared or HD), BF),
            pltpu.SemaphoreType.DMA((3,)),
        ],
        out_space=pl.ANY,
        flops=4 * span * width * late_start,
        nbytes=late_start * (4 * width + 2 * span),
    )
    return (
        query_grad[None, None],
        dk_past[None, None],
        dv_past[None, None],
        dkw[None],
        dvw[None],
        section_grad[None, None],
    )


def solution(mesh):
    return jax.shard_map(
        on_device,
        mesh=mesh,
        in_specs=(
            P("pipe", "dp", None, "tensor"),
            P("pipe", "dp", None, "tensor"),
            P("pipe", "dp", "tensor", None),
            P("pipe", "dp", "tensor", None),
            P("pipe", "dp", "tensor", None),
            P("pipe", "dp", "tensor", None),
            P("pipe", "dp", None, "tensor"),
            P("pipe", "tensor", None),
            P("pipe", "tensor", None),
            P("pipe", "dp"),
        ),
        out_specs=(
            P("pipe", "dp", None, "tensor"),
            P("pipe", "dp", "tensor", None),
            P("pipe", "dp", "tensor", None),
            P("pipe", "tensor", "dp"),
            P("pipe", "tensor", "dp"),
            P("pipe", "dp", None, "tensor"),
        ),
        check_vma=False,
    )
```

```python
import functools

import jax
import jax.numpy as jnp
import numpy as np
from jax import lax
from jax.experimental import pallas as pl
from jax.experimental.pallas import tpu as pltpu
from jax.sharding import PartitionSpec as P

HD = 128
rope_base = 500000.0
neg_large = -1e30
log2_e = 1.4426950408889634
BF = jnp.bfloat16
F32 = jnp.float32
VMEM = pltpu.VMEM

AHEAD, SHARED = 6, 5


def call(body, out_shape, args, scratch=(), flops=0, nbytes=0, specs=None, limit=40, out_space=VMEM):
    return pl.pallas_call(
        body,
        out_shape=out_shape,
        in_specs=specs or [pl.BlockSpec(memory_space=VMEM)] * len(args),
        out_specs=jax.tree.map(lambda _: pl.BlockSpec(memory_space=out_space), out_shape),
        scratch_shapes=list(scratch),
        compiler_params=pltpu.CompilerParams(vmem_limit_bytes=limit * 1024 * 1024),
        cost_estimate=pl.CostEstimate(flops=flops, bytes_accessed=nbytes, transcendentals=0),
    )(*args)


def shape(rows, columns, dtype):
    return jax.ShapeDtypeStruct((rows, columns), dtype)


def swap(block, axis, distance):
    size = lax.axis_size(axis)
    return lax.ppermute(block, axis, [(i, i ^ distance) for i in range(size)])


def from_next_section(block):
    size = lax.axis_size("pipe")
    return lax.ppermute(block, "pipe", [(i, (i - 1) % size) for i in range(size)])


def after(block, *events):
    return lax.optimization_barrier((block, *events))[0]


def head_columns(head):
    return pl.ds(pl.multiple_of(head * HD, HD), HD)


def my_place(copies):
    me = lax.axis_index("tensor")
    return me // 2, me % 2, me // copies


def load_all(sources, targets, arrived):
    loads = [
        pltpu.make_async_copy(source, target, arrived.at[i])
        for i, (source, target) in enumerate(zip(sources, targets))
    ]
    for load in loads:
        load.start()
    for load in loads:
        load.wait()


def pack_body(heads, copies, *refs):
    z, core, own = my_place(copies)
    outs, held, arrived = refs[4 : 4 + heads], refs[4 + heads : 8 + heads], refs[-1]
    load_all(refs[:4], held, arrived)
    pk, pv, sk, sv = held
    rows = pk.shape[0]
    for apart in range(heads):
        columns = head_columns(own ^ apart)
        outs[apart][:rows, :HD] = pk[:, columns]
        outs[apart][:rows, HD:] = pv[:, columns]
        outs[apart][rows:, :HD] = sk[:, columns]
        outs[apart][rows:, HD:] = sv[:, columns]


def ahead_body(kw, vw, weights, arrived):
    ahead = weights.shape[0] // 2
    count = arrived.shape[0] // 2
    rows = ahead // count
    sources = [array.at[pl.ds(i * rows, rows)] for array in (kw, vw) for i in range(count)]
    targets = [weights.at[pl.ds(i * rows, rows)] for i in range(2 * count)]
    load_all(sources, targets, arrived)


def table_body(chips, past_rows, span_rows, offset, freq, cos, sin, first):
    me = lax.axis_index("tensor")
    z, core = me // 2, me % 2
    places = 2 * chips
    start = offset[0, 0]
    frequencies = freq[...]
    place = lax.broadcasted_iota(jnp.int32, (places, HD), 0)
    holder = 2 * (z ^ (place % chips)) + (core ^ (place // chips))
    row = lax.broadcasted_iota(jnp.int32, (max(past_rows, span_rows), HD), 0)
    lane = lax.broadcasted_iota(jnp.int32, row.shape, 1)

    def turn(positions):
        angles = positions.astype(F32) * frequencies
        return jnp.cos(angles), jnp.sin(angles)

    row_cos, row_sin = turn(row)
    for low, rows, begin in ((0, past_rows, 0), (places * past_rows, span_rows, start)):
        place_cos, place_sin = turn(begin + rows * holder)
        signs = jnp.where(lane[:rows] < HD // 2, -1.0, 1.0)
        for i in range(places):
            part = slice(low + i * rows, low + (i + 1) * rows)
            c, s = place_cos[i : i + 1], place_sin[i : i + 1]
            cos[part, :] = c * row_cos[:rows] - s * row_sin[:rows]
            sin[part, :] = (s * row_cos[:rows] + c * row_sin[:rows]) * signs
            index = rows * (2 * (z ^ (i % chips)) + (core ^ (i // chips))) + row[:rows]
            first[part, :] = jnp.where(index < start, -1, 1 << 30) if low == 0 else index


def attend_body(chips, past_rows, span_rows, q, do, cos, sin, first, *refs):
    pieces = refs[: 2 * chips]
    dq, keep, send, kr, krt, v, at, dst, qs, ds = refs[2 * chips :]
    span = q.shape[0]
    heads = q.shape[1] // HD
    past = 2 * chips * past_rows
    keys = past + 2 * chips * span_rows
    scale = HD**-0.5
    for place in range(2 * chips):
        piece = pieces[place]
        for start, count, lower in (
            (place * past_rows, past_rows, 0),
            (past + place * span_rows, span_rows, past_rows),
        ):
            rows = slice(start, start + count)
            k = piece[lower : lower + count, :HD].astype(F32)
            turned = k * cos[rows, :] + pltpu.roll(k, HD // 2, 1) * sin[rows, :]
            kr[rows, :] = turned.astype(BF)
            v[rows, :] = piece[lower : lower + count, HD:]
    krt[...] = kr[...].T
    for h in range(heads):
        qs[h * span : (h + 1) * span, :] = q[:, h * HD : (h + 1) * HD]
        ds[h * span : (h + 1) * span, :] = do[:, h * HD : (h + 1) * HD]
    row = lax.broadcasted_iota(jnp.int32, (keys, span), 1)
    start_key = jnp.concatenate([first[...]] * (span // HD), axis=1)
    visible = start_key <= row
    contract_last = (((1,), (1,)), ((), ()))

    def products(h):
        columns = slice(h * span, (h + 1) * span)
        s = lax.dot_general(kr[...], qs[columns, :], contract_last, preferred_element_type=F32)
        dp = lax.dot_general(v[...], ds[columns, :], contract_last, preferred_element_type=F32)
        return s, dp

    following = products(0)
    for h in range(heads):
        columns = slice(h * span, (h + 1) * span)
        s, dp = following
        if h + 1 < heads:
            following = products(h + 1)
        s = jnp.where(visible, s * (scale * log2_e), neg_large)
        e = jnp.exp2(s - jnp.max(s, axis=0, keepdims=True))
        a = e * (1.0 / jnp.sum(e, axis=0, keepdims=True))
        a_bf = a.astype(BF)
        at[:, columns] = a_bf
        delta = jnp.sum(a_bf.astype(F32) * dp, axis=0, keepdims=True)
        d = (a * (dp - delta)).astype(BF)
        dst[:, columns] = d
        dqt = jnp.dot(krt[...], d, preferred_element_type=F32) * scale
        dq[:, h * HD : (h + 1) * HD] = dqt.astype(BF).T
    dk = jnp.dot(dst[...], qs[...], preferred_element_type=F32) * scale
    dk = dk * cos[...] - pltpu.roll(dk, HD // 2, 1) * sin[...]
    dv = jnp.dot(at[...], ds[...], preferred_element_type=F32)
    half = chips * past_rows
    quarter = chips * span_rows
    for columns, grad in ((slice(0, HD), dk), (slice(HD, 2 * HD), dv)):
        keep[:half, columns] = grad[:half]
        keep[half:, columns] = grad[past : past + quarter]
        send[:half, columns] = grad[half:past].astype(BF)
        send[half:, columns] = grad[past + quarter :].astype(BF)


def chip_sum_body(chips, past_rows, keep, received, span_own, span_send, *past):
    half = chips * past_rows
    total = keep[...] + received[...].astype(F32)
    span_own[...] = total[half:]
    span_send[...] = total[half:].astype(BF)
    for j in range(chips):
        block = total[j * past_rows : (j + 1) * past_rows]
        past[j][...] = block.astype(past[j].dtype)


def sum_span(heads, copies, chips, span_rows, blocks, ordered, span_grad):
    z, core, head = my_place(copies)
    per_head = copies // 2
    width = heads * HD
    for apart in range(heads):
        total = [None] * chips
        for j in range(apart * per_head, (apart + 1) * per_head):
            for i in range(chips):
                part = blocks[j][i * span_rows : (i + 1) * span_rows, :].astype(F32)
                total[i ^ j] = part if total[i ^ j] is None else total[i ^ j] + part
        key_columns = head_columns(head ^ apart)
        value_columns = pl.ds(pl.multiple_of(width + (head ^ apart) * HD, HD), HD)
        for i in range(chips):
            rows = pl.ds(pl.multiple_of((z ^ i) * span_rows, span_rows), span_rows)
            rounded = total[i].astype(ordered.dtype)
            ordered[rows, key_columns] = rounded[:, :HD]
            ordered[rows, value_columns] = rounded[:, HD:]
    span_grad[...] = ordered[...].astype(BF)


def span_sum_body(heads, copies, chips, span_rows, peers, *refs):
    blocks = refs[:chips]
    span_grad = refs[chips]
    sends, ordered = refs[chips + 1 : -1], refs[-1]
    sum_span(heads, copies, chips, span_rows, blocks, ordered, span_grad)
    replica = lax.axis_index("dp")
    width = heads * HD
    share = width // peers
    for k, target in enumerate(sends, 1):
        lower = pl.multiple_of((replica ^ k) * share, HD)
        target[:, :share] = span_grad[:, pl.ds(lower, share)]
        target[:, share:] = span_grad[:, pl.ds(pl.multiple_of(width + lower, HD), share)]


def past_sum_body(heads, copies, *refs):
    blocks = refs[:-2]
    dk_past, dv_past = refs[-2:]
    z, core, head = my_place(copies)
    per_head = copies // 2
    for apart in range(heads):
        total = blocks[apart * per_head][...].astype(F32)
        for j in range(apart * per_head + 1, (apart + 1) * per_head):
            total = total + blocks[j][...].astype(F32)
        columns = head_columns(head ^ apart)
        dk_past[:, columns] = total[:, :HD]
        dv_past[:, columns] = total[:, HD:]


def row_type(span_rows):
    return BF if span_rows % 16 == 0 else F32


def weave(chips, span_rows, target, own, other):
    core = lax.axis_index("tensor") % 2
    for z in range(chips):
        part = slice(z * span_rows, (z + 1) * span_rows)
        lower = pl.multiple_of((2 * z + core) * span_rows, span_rows)
        target[pl.ds(lower, span_rows), :] = own[part, :].astype(target.dtype)
        lower = pl.multiple_of((2 * z + 1 - core) * span_rows, span_rows)
        target[pl.ds(lower, span_rows), :] = other[part, :].astype(target.dtype)


def late_grad_body(chips, span_rows, own, other, kw, vw, out, rows):
    weave(chips, span_rows, rows, own, other)
    width = kw.shape[1]
    contract_last = (((1,), (1,)), ((), ()))
    total = lax.dot_general(
        rows[:, :width].astype(BF), kw[...], contract_last, preferred_element_type=F32
    )
    total = total + lax.dot_general(
        rows[:, width:].astype(BF), vw[...], contract_last, preferred_element_type=F32
    )
    out[...] = total.astype(BF)


def early_grad_body(chips, span_rows, sections, ahead, own, other, weights, late, *refs):
    more, (out, rows, held, held_more, moved) = refs[:-5], refs[-5:]
    last = lax.axis_index("pipe") == sections - 1
    width = weights.shape[1]
    features = held.shape[1]
    ready = features - late.shape[1]
    contract_last = (((1,), (1,)), ((), ()))

    def move(source, low, high, which):
        columns = pl.ds(low, high - low)
        return pltpu.make_async_copy(source, out.at[:, columns], moved.at[which])

    @pl.when(last)
    def _():
        held[...] = jnp.zeros_like(held)
        whole = move(held, 0, features, 0)
        whole.start()
        whole.wait()

    @pl.when(jnp.logical_not(last))
    def _():
        moves = [move(late, ready, features, 0)]
        moves[0].start()
        weave(chips, span_rows, rows, own, other)
        kind = lax.axis_index("dp") if more else 0

        def product(which, block):
            columns = pl.ds(pl.multiple_of(which * width, HD), width)
            grad = rows[:, columns].astype(BF)
            return lax.dot_general(grad, block, contract_last, preferred_element_type=F32)

        total = product(kind, weights[:ahead]) + product(1 - kind, weights[ready:])
        held[:, :ahead] = total.astype(BF)
        moves.append(move(held.at[:, pl.ds(0, ahead)], 0, ahead, 1))
        moves[1].start()
        if more:
            total = product(kind, weights[ahead:ready]) + product(1 - kind, more[0][...])
            held_more[...] = total.astype(BF)
            moves.append(move(held_more, ahead, ready, 2))
            moves[2].start()
        for each in moves:
            each.wait()


def weight_grad_body(chips, span_rows, replicas, *refs):
    count = replicas - 1
    normed = refs[:replicas]
    span_grad, other_grad = refs[replicas : replicas + 2]
    own = refs[replicas + 2 : replicas + 2 + count]
    other = refs[replicas + 2 + count : replicas + 2 + 2 * count]
    dkw, dvw, mine, rows = refs[replicas + 2 + 2 * count :]
    share = dkw.shape[1]
    width = span_grad.shape[1] // 2
    weave(chips, span_rows, mine, span_grad, other_grad)
    lower = pl.multiple_of(lax.axis_index("dp") * share, HD)
    grads = [
        jnp.concatenate(
            [mine[:, pl.ds(half * width + lower, share)].astype(BF) for half in range(2)], axis=1
        )
    ]
    for k in range(count):
        weave(chips, span_rows, rows.at[k], own[k], other[k])
        grads.append(rows[k].astype(BF))
    contract_first = (((0,), (0,)), ((), ()))
    total = None
    for block, grad in zip(normed, grads):
        product = lax.dot_general(block[...], grad, contract_first, preferred_element_type=F32)
        product = product.astype(BF).astype(F32)
        total = product if total is None else total + product
    dkw[...] = total[:, :share]
    dvw[...] = total[:, share:]


def on_device(
    queries,
    grad_out,
    past_keys,
    past_values,
    span_keys,
    span_values,
    normed,
    key_weight,
    value_weight,
    offsets,
):
    devices = lax.axis_size("tensor")
    replicas = lax.axis_size("dp")
    chips = devices // 2
    past_rows = past_keys.shape[2]
    span_rows = span_keys.shape[2]
    span = queries.shape[2]
    width = past_keys.shape[3]
    heads = width // HD
    copies = devices // heads
    features = normed.shape[3]
    share = width // replicas
    keys = devices * (past_rows + span_rows)
    local_heads = queries.shape[3] // HD

    normed_rows = normed[0, 0]
    kw, vw = key_weight[0], value_weight[0]
    ahead, shared = features * AHEAD // 16, features * SHARED // 16
    if replicas != 2:
        ahead, shared = (ahead + shared // 2) // HD * HD, 0
    late_start = ahead + shared

    packed = call(
        functools.partial(pack_body, heads, copies),
        [shape(past_rows + span_rows, 2 * HD, BF)] * heads,
        (past_keys[0, 0], past_values[0, 0], span_keys[0, 0], span_values[0, 0]),
        nbytes=2 * (past_rows + span_rows) * 2 * width * 2,
        scratch=[VMEM((past_rows, width), BF)] * 2
        + [VMEM((span_rows, width), BF)] * 2
        + [pltpu.SemaphoreType.DMA((4,))],
        specs=[pl.BlockSpec(memory_space=pltpu.HBM)] * 4,
    )
    per_head = copies // 2
    half_dim = HD // 2
    freq = np.tile(rope_base ** (-2.0 * np.arange(half_dim) / HD), 2).astype(np.float32)
    cos, sin, first = call(
        functools.partial(table_body, chips, past_rows, span_rows),
        [shape(keys, HD, F32)] * 2 + [shape(keys, HD, jnp.int32)],
        (offsets, jnp.asarray(freq[None])),
        nbytes=keys * HD * 12,
        specs=[pl.BlockSpec(memory_space=pltpu.SMEM), pl.BlockSpec(memory_space=VMEM)],
    )
    pieces = [swap(packed[j // per_head], "tensor", 2 * j) for j in range(1, chips)]
    late_kw, late_vw, cos, *near = lax.optimization_barrier(
        (
            after(kw, packed[0])[late_start:],
            after(vw, packed[0])[late_start:],
            cos,
            packed[0],
            *pieces[:-1],
        )
    )
    pieces = [*near, pieces[-1]]
    pieces = pieces + [swap(piece, "tensor", 1) for piece in pieces]

    ready = [kw[:late_start], vw[:ahead]]
    if shared:
        first_half = lax.axis_index("dp") == 0
        ready = [
            jnp.where(first_half, kw[:late_start], vw[:late_start]),
            jnp.where(first_half, vw[:ahead], kw[:ahead]),
        ]
    weights = from_next_section(jnp.concatenate(ready, axis=0))
    normed_from = [swap(normed_rows, "dp", k) for k in range(1, replicas)]

    part_rows = chips * (past_rows + span_rows)
    query_grad, keep, send = call(
        functools.partial(attend_body, chips, past_rows, span_rows),
        [
            shape(span, local_heads * HD, BF),
            shape(part_rows, 2 * HD, F32),
            shape(part_rows, 2 * HD, BF),
        ],
        (queries[0, 0], grad_out[0, 0], cos, sin, first, *pieces),
        scratch=[
            VMEM((keys, HD), BF),
            VMEM((HD, keys), BF),
            VMEM((keys, HD), BF),
            VMEM((keys, local_heads * span), BF),
            VMEM((keys, local_heads * span), BF),
            VMEM((local_heads * span, HD), BF),
            VMEM((local_heads * span, HD), BF),
        ],
        flops=10 * keys * local_heads * span * HD,
        nbytes=4 * span * local_heads * HD * 2,
    )
    span_own, span_send, *past = call(
        functools.partial(chip_sum_body, chips, past_rows),
        [
            shape(chips * span_rows, 2 * HD, F32),
            shape(chips * span_rows, 2 * HD, BF),
            shape(past_rows, 2 * HD, F32),
        ]
        + [shape(past_rows, 2 * HD, BF)] * (chips - 1),
        (keep, swap(send, "tensor", 1)),
        nbytes=part_rows * 2 * HD * 8,
    )
    received = [swap(span_send, "tensor", 2 * j) for j in range(1, chips)]
    span_grad, *shares = call(
        functools.partial(span_sum_body, heads, copies, chips, span_rows, replicas),
        [shape(chips * span_rows, 2 * width, BF)]
        + [shape(chips * span_rows, 2 * share, BF)] * (replicas - 1),
        (after(span_own, weights, *normed_from), *received),
        scratch=[VMEM((chips * span_rows, 2 * width), row_type(span_rows))],
        nbytes=part_rows * 2 * HD * 8,
    )
    share_from = [swap(block, "dp", k + 1) for k, block in enumerate(shares)]
    next_grad = from_next_section(span_grad)
    past = past[:1] + [swap(after(past[j], span_grad if j <= 2 else next_grad), "tensor", 2 * j) for j in range(1, chips)]
    other_grad = swap(span_grad, "tensor", 1)
    dkw, dvw = call(
        functools.partial(weight_grad_body, chips, span_rows, replicas),
        [shape(features, share, F32)] * 2,
        (
            normed_rows,
            *normed_from,
            span_grad,
            other_grad,
            *share_from,
            *[swap(after(part, *normed_from), "tensor", 1) for part in share_from],
        ),
        scratch=[
            VMEM((span, 2 * width), row_type(span_rows)),
            VMEM((replicas - 1, span, 2 * share), row_type(span_rows)),
        ],
        flops=4 * span * features * share * replicas,
        nbytes=features * (2 * span * replicas + 8 * share),
    )
    dk_past, dv_past = call(
        functools.partial(past_sum_body, heads, copies),
        [shape(past_rows, width, F32)] * 2,
        past,
        nbytes=chips * past_rows * 2 * HD * 4,
    )
    late = call(
        functools.partial(late_grad_body, chips, span_rows),
        shape(span, features - late_start, BF),
        (
            span_grad,
            other_grad,
            late_kw,
            late_vw,
        ),
        scratch=[VMEM((span, 2 * width), row_type(span_rows))],
        flops=4 * span * width * (features - late_start),
        nbytes=(features - late_start) * (4 * width + 2 * span),
    )
    more = [swap(after(weights, *share_from)[ahead:late_start], "dp", 1)] if shared else []
    late = from_next_section(after(late, next_grad, past[1], past[2], *share_from))
    section_grad = call(
        functools.partial(early_grad_body, chips, span_rows, lax.axis_size("pipe"), ahead),
        shape(span, features, BF),
        (next_grad, swap(next_grad, "tensor", 1), weights, late, *more),
        scratch=[
            VMEM((span, 2 * width), row_type(span_rows)),
            VMEM((span, features), BF),
            VMEM((span, shared or HD), BF),
            pltpu.SemaphoreType.DMA((3,)),
        ],
        out_space=pl.ANY,
        flops=4 * span * width * late_start,
        nbytes=late_start * (4 * width + 2 * span),
    )
    return (
        query_grad[None, None],
        dk_past[None, None],
        dv_past[None, None],
        dkw[None],
        dvw[None],
        section_grad[None, None],
    )


def solution(mesh):
    return jax.shard_map(
        on_device,
        mesh=mesh,
        in_specs=(
            P("pipe", "dp", None, "tensor"),
            P("pipe", "dp", None, "tensor"),
            P("pipe", "dp", "tensor", None),
            P("pipe", "dp", "tensor", None),
            P("pipe", "dp", "tensor", None),
            P("pipe", "dp", "tensor", None),
            P("pipe", "dp", None, "tensor"),
            P("pipe", "tensor", None),
            P("pipe", "tensor", None),
            P("pipe", "dp"),
        ),
        out_specs=(
            P("pipe", "dp", None, "tensor"),
            P("pipe", "dp", "tensor", None),
            P("pipe", "dp", "tensor", None),
            P("pipe", "tensor", "dp"),
            P("pipe", "tensor", "dp"),
            P("pipe", "dp", None, "tensor"),
        ),
        check_vma=False,
    )
```
